256 devices in a mesh: dp: 32 (over y, x, core), seq: 8 (over z).
Axes of the slice: x: 4, y: 4, z: 8, core: 2. Of those that a mesh axis runs over, the one named last changes fastest.
Arguments:
- streams: bfloat16 [32, 1024, 12288], P('dp', 'seq'), may hold values from -6 to 6
- short_filter: bfloat16 [7, 12288], P(None, 'dp'), may hold values from -2 to 2
- long_filter: bfloat16 [256, 128], P('dp'), may hold values from -0.5 to 0.5
- skip: bfloat16 [4096], P('dp'), may hold values from 0.5 to 1.5
- grad_out: bfloat16 [32, 1024, 4096], P('dp', 'seq'), may hold values from -6 to 6
Outputs:
- grad_streams: bfloat16 [32, 1024, 12288], P('dp', 'seq')
- grad_short: float32 [7, 12288], P(None, 'dp')
- grad_long: float32 [256, 128], P('dp')
- grad_skip: float32 [4096], P('dp')
The draws below stay inside these ranges and needn't reach their ends.
All inputs are finite; a program needn't handle non-finite values.
Results may differ from the reference program's by a relative error of at most 0.01.
Values may be sent and summed in bfloat16 or wider, within the bound.
No kernel may reach another device: no remote copies, remote signals or barrier semaphores. Data moves between devices by JAX's collectives and lax.ppermute only.
A program may use at most 192 MiB of HBM per device.

```python
import math
import jax
import jax.numpy as jnp
from jax import lax

CHAN = 4096
GROUP = 16
FILT = 128
SHORT = 7
GROUPS = 256
SEQ_LEN = 1024
SEQS = 32
N_DP = 32


def with_spikes(drawn, key, source, target, blocks, factor):
    owner, partner = [(jnp.arange(drawn.shape[position]) // (drawn.shape[position] // blocks)).reshape([-1 if axis == position else 1 for axis in range(drawn.ndim)]) for position in (source, target)]
    chosen = jax.random.permutation(key, blocks)[partner]
    strong = (owner == chosen) | (owner == (partner + blocks // 2) % blocks)
    return jnp.where(strong, factor * drawn, drawn)


def steps_of(rng, extent, shards, low, top_value):
    def one(axis_at, shards_of):
        steps = jax.random.uniform(jax.random.fold_in(jax.random.fold_in(rng, 6), axis_at), (shards_of,), jnp.float32, low / len(shards), top_value / len(shards))
        return jnp.repeat(jnp.exp(steps), extent[axis_at] // shards_of).reshape((-1,) + (1,) * (len(extent) - axis_at - 1))

    loudness = one(*shards[0])
    for cut in shards[1:]:
        loudness = loudness * one(*cut)
    return loudness


def centred(stream_key, dims, width, most, cuts=(), kind=jnp.bfloat16):
    values = jax.random.normal(stream_key, dims, jnp.float32) * width
    if len(cuts) > 0:
        values = steps_of(stream_key, dims, cuts, -0.22, 0.18) * values
    return jnp.clip(values, min=-most, max=most).astype(kind)


def heavy_noise(own_key, dims, width, reach, cuts, heavy, held_as=jnp.bfloat16):
    array = width * jax.random.normal(own_key, dims, jnp.float32)
    if cuts:
        array = array * steps_of(own_key, dims, cuts, -0.22, 0.18)
    return jnp.clip(with_spikes(array, jax.random.fold_in(own_key, 3), *heavy), -reach, reach).astype(held_as)


def setup_inputs(seed: int = 0) -> dict:
    arg_keys = jax.random.split(jax.random.key(seed), 6)
    streams = centred(arg_keys[0], (SEQS, SEQ_LEN, 3 * CHAN), 1.0, 6.0, ((0, 32), (1, 8)))
    short_filter = centred(arg_keys[1], (SHORT, 3 * CHAN), SHORT ** -0.5, 2.0, ((1, 32),))
    long_filter = centred(arg_keys[2], (GROUPS, FILT), FILT ** -0.5, 0.5, ((0, 32),))
    skip = jnp.clip(0.5 + 1.0 * jax.random.uniform(arg_keys[3], (CHAN,), jnp.float32) ** steps_of(arg_keys[3], (CHAN,), ((0, 32),), -0.2, 0.2), 0.5, 1.5).astype(jnp.bfloat16)
    grad_out = heavy_noise(arg_keys[4], (SEQS, SEQ_LEN, CHAN), 1.0, 6.0, ((0, 32), (1, 8)), (0, 2, 32, 2.75))
    return {"streams": streams, "short_filter": short_filter, "long_filter": long_filter, "skip": skip, "grad_out": grad_out}


def block_windows(signal):
    seq_rows, chan_width = signal.shape
    block_count = seq_rows // FILT
    padded = jnp.concatenate([jnp.zeros((FILT, chan_width), signal.dtype), signal], axis=0)
    blocks = padded.reshape(block_count + 1, FILT, chan_width)
    return jnp.concatenate([blocks[:-1], blocks[1:]], axis=1)[:, 1:, :]

def toeplitz(filters, tok_rows):
    group_count, long_taps = filters.shape
    span_cols = tok_rows + long_taps - 1
    kernel_line = jnp.concatenate([filters[:, ::-1], jnp.zeros((group_count, tok_rows), filters.dtype)], axis=1)
    tiled = jnp.tile(kernel_line, (1, tok_rows))[:, :tok_rows * span_cols]
    return tiled.reshape(group_count, tok_rows, span_cols)

def diagonal_sums(correlation, long_taps):
    group_count, tok_rows, span_cols = correlation.shape
    flat_corr = correlation.reshape(group_count, tok_rows * span_cols)
    flat_corr = jnp.concatenate([flat_corr, jnp.zeros((group_count, tok_rows), correlation.dtype)], axis=1)
    skewed = flat_corr.reshape(group_count, tok_rows, span_cols + 1)[:, :, :long_taps]
    return lax.optimization_barrier(jnp.sum(skewed, axis=1))[:, ::-1]

def causal_long(signal, matrix):
    seq_rows, chan_width = signal.shape
    windows = block_windows(signal)
    group_count = matrix.shape[0]
    block_count, span_cols, _ = windows.shape
    shaped = windows.reshape(block_count, span_cols, group_count, chan_width // group_count)
    result = jnp.einsum('gsm,cmgk->csgk', matrix, shaped)
    return result.reshape(seq_rows, chan_width)

def lag_products(left_side, signal):
    windows = block_windows(signal)
    block_count, span_cols, chan_width = windows.shape
    group_count = chan_width // GROUP
    pieces = left_side.reshape(block_count, FILT, group_count, GROUP)
    correlation = jnp.einsum('csgk,cmgk->gsm', pieces, windows.reshape(block_count, span_cols, group_count, GROUP))
    return diagonal_sums(correlation, FILT)

def causal_short(signal, filters):
    seq_rows = signal.shape[0]
    padded = jnp.concatenate([jnp.zeros((SHORT - 1, signal.shape[1]), signal.dtype), signal], axis=0)
    running = filters[0] * signal
    for lag_step in range(1, SHORT):
        running = running + filters[lag_step] * padded[SHORT - 1 - lag_step:SHORT - 1 - lag_step + seq_rows]
    return running

def reference(streams, short_filter, long_filter, skip, grad_out):
    short_vals = short_filter.astype(jnp.float32)
    long_vals = long_filter.astype(jnp.float32)
    skip_vals = skip.astype(jnp.float32)
    matrix = toeplitz(long_vals, FILT)
    chan_width = grad_out.shape[2]
    seq_rows = streams.shape[1]

    def one_sequence(totals, pair_item):
        inputs, cotangent_in = pair_item
        source = inputs.astype(jnp.float32)
        mixed = causal_short(source, short_vals)
        query_feat = mixed[:, :chan_width]
        key_feat = mixed[:, chan_width:2 * chan_width]
        value_feat = mixed[:, 2 * chan_width:]
        product = (key_feat * value_feat).astype(jnp.bfloat16)
        product_vals = product.astype(jnp.float32)
        wave = causal_long(product_vals, matrix) + skip_vals * product_vals
        cotangent = cotangent_in.astype(jnp.float32)
        gate_grad = (cotangent * query_feat).astype(jnp.bfloat16)
        gate_vals = gate_grad.astype(jnp.float32)
        prod_grad = causal_long(gate_vals[::-1], matrix)[::-1] + skip_vals * gate_vals
        mixed_grad = jnp.concatenate([cotangent * wave, prod_grad * value_feat, prod_grad * key_feat], axis=1)
        input_grad = causal_short(mixed_grad[::-1], short_vals)[::-1].astype(jnp.bfloat16)
        padded = jnp.concatenate([jnp.zeros((SHORT - 1, source.shape[1]), source.dtype), source], axis=0)
        short_terms = jnp.stack([lax.optimization_barrier(jnp.sum(mixed_grad * padded[SHORT - 1 - lag_step:SHORT - 1 - lag_step + seq_rows], axis=0)) for lag_step in range(SHORT)], axis=0)
        long_terms = lag_products(gate_vals, product_vals)
        skip_terms = lax.optimization_barrier(jnp.sum(gate_vals * product_vals, axis=0))
        return ((totals[0] + short_terms, totals[1] + long_terms, totals[2] + skip_terms), input_grad)
    start = (jnp.zeros((SHORT, 3 * chan_width), jnp.float32), jnp.zeros((chan_width // GROUP, FILT), jnp.float32), jnp.zeros((chan_width,), jnp.float32))
    totals, grad_streams = lax.scan(one_sequence, start, (streams, grad_out))
    scale = 1.0 / math.sqrt(N_DP * SEQ_LEN)
    return (grad_streams, totals[0] * scale, totals[1] * scale, totals[2] * scale)
```

```python
import functools
import math

import jax
import jax.numpy as jnp
from jax import lax
from jax.experimental import pallas as pl
from jax.experimental.pallas import tpu as pltpu
from jax.sharding import PartitionSpec as P

LANES = 128
GROUP = 16
SHORT = 7
ROWS = 128
PIECE = 16
SPAN = PIECE + 128
BF = jnp.bfloat16
F32 = jnp.float32


def params(mib):
    return pltpu.CompilerParams(vmem_limit_bytes=mib * 1024 * 1024)


def whole():
    return pl.BlockSpec(memory_space=pltpu.VMEM)


def anywhere():
    return pl.BlockSpec(memory_space=pl.ANY)


def pack_kernel(short_ref, long_ref, skip_ref, streams_ref, out_ref, tail_ref, sem):
    copy = pltpu.make_async_copy(streams_ref.at[0, pl.ds(ROWS - 16, 16), :], tail_ref, sem)
    copy.start()
    short = short_ref[...].astype(F32)
    skip = skip_ref[...].astype(F32)
    nothing = jnp.zeros((1, LANES), F32)
    rows = []
    for part in range(3):
        rows.append(short[:, part * LANES : (part + 1) * LANES])
        rows.append(skip if part == 0 else nothing)
    packed = jnp.concatenate(rows + [long_ref[...].astype(F32)], axis=0).astype(BF)
    out_ref[...] = jnp.broadcast_to(packed[None], out_ref.shape)
    copy.wait()


def pack(short_filter, long_filter, skip, streams, shards):
    return pl.pallas_call(
        pack_kernel,
        out_shape=(
            jax.ShapeDtypeStruct((shards, 32, LANES), BF),
            jax.ShapeDtypeStruct((16, streams.shape[2]), BF),
        ),
        in_specs=[whole(), whole(), whole(), anywhere()],
        out_specs=(whole(), anywhere()),
        scratch_shapes=[pltpu.SemaphoreType.DMA],
        compiler_params=params(16),
        name="pack",
    )(short_filter, long_filter, skip[None], streams)


def taps_of(table, tile):
    return table[tile // 3, pl.ds(pl.multiple_of(tile % 3 * 8, 8), 8), :]


def gates_kernel(
    first_tile, tiles, count, g_ref, sq, sk, sv, hq, hk, hv, cot, prod, gate, key, val, table, ext
):
    step = pl.program_id(0)

    @pl.when(step == 0)
    def _():
        table[...] = g_ref[...].astype(F32)

    for t in range(tiles):
        tile = first_tile + step * tiles + t
        cols = slice(t * LANES, (t + 1) * LANES)
        mixed = []
        for part, (source, halo) in enumerate(((sq, hq), (sk, hk), (sv, hv))):
            taps = taps_of(table, tile + part * count)
            slot = ext.at[t % 2, part]
            slot[0:8, :] = halo[:, cols].astype(F32)[8:16]
            slot[8 : 8 + ROWS, :] = source[0, :, cols].astype(F32)
            running = taps[0:1] * slot[8 : 8 + ROWS, :]
            for lag in range(1, SHORT):
                running = running + taps[lag : lag + 1] * slot[8 - lag : 8 - lag + ROWS, :]
            mixed.append(running)
        prod[:, cols] = (mixed[1] * mixed[2]).astype(BF)
        gate[:, cols] = (cot[0, :, cols].astype(F32) * mixed[0]).astype(BF)
        key[:, cols] = mixed[1].astype(BF)
        val[:, cols] = mixed[2].astype(BF)


def gates(first, width, gathered, streams, before, grad_out):
    count = grad_out.shape[2] // LANES
    step_width = min(width, 512)
    steps = width // step_width
    tiles = step_width // LANES
    blocks = grad_out.shape[2] // step_width
    lead = first // step_width

    def stream(part):
        return pl.BlockSpec((1, ROWS, step_width), lambda i: (0, 0, part * blocks + lead + i))

    def halo(part):
        return pl.BlockSpec((16, step_width), lambda i: (0, part * blocks + lead + i))

    out = jax.ShapeDtypeStruct((ROWS, width), BF)
    out_spec = pl.BlockSpec((ROWS, step_width), lambda i: (0, i))
    return pl.pallas_call(
        functools.partial(gates_kernel, first // LANES, tiles, count),
        grid=(steps,),
        out_shape=(out,) * 4,
        in_specs=[pl.BlockSpec(gathered.shape, lambda i: (0, 0, 0))]
        + [stream(part) for part in range(3)]
        + [halo(part) for part in range(3)]
        + [pl.BlockSpec((1, ROWS, step_width), lambda i: (0, 0, lead + i))],
        out_specs=(out_spec,) * 4,
        scratch_shapes=[
            pltpu.VMEM(gathered.shape, F32),
            pltpu.VMEM((2, 3, 8 + ROWS, LANES), F32),
        ],
        compiler_params=params(40),
        cost_estimate=pl.CostEstimate(
            flops=60 * 3 * ROWS * width, bytes_accessed=16 * ROWS * width, transcendentals=0
        ),
        name="gates",
    )(gathered, streams, streams, streams, before, before, before, grad_out)


def windows(block, pair):
    low = 2 * PIECE * pair
    return jnp.concatenate(
        [block[low : low + SPAN], block[low + PIECE : low + PIECE + SPAN]], axis=1
    )


def picked(result, owner):
    out = result[0:PIECE]
    for g in range(1, LANES // GROUP):
        out = jnp.where(owner == g, result[g * PIECE : (g + 1) * PIECE], out)
    return out


def toeplitz_rows(filters, shift):
    pieces = []
    for g in range(LANES // GROUP):
        line = jnp.concatenate([filters[g : g + 1], jnp.zeros((1, LANES), F32)], axis=1)
        line = jnp.broadcast_to(line, (PIECE, 2 * LANES))
        pieces.append(pltpu.roll(line, shift, 1, stride=1, stride_axis=0))
    return jnp.concatenate(pieces, axis=0).astype(BF)[:, :SPAN]


def back_kernel(
    first_tile, tiles, count, chained, g_ref, sq, sk, sv, hq, hk, hv, cot, prod, prior, gate, ahead, key, val, *rest
):
    if chained:
        rest = rest[1:]
    gs_ref, tail_ref, head_ref, short_ref, long_ref, table, mixed, corr, held, sems = rest
    step = pl.program_id(0)
    steps = pl.num_programs(0)
    slot = lax.rem(step, 2)
    width = tiles * LANES
    groups = LANES // GROUP

    def copies(at_step, at_slot):
        return [
            pltpu.make_async_copy(
                held.at[at_slot, part],
                gs_ref.at[0, :, pl.ds(pl.multiple_of((part * count + first_tile + at_step * tiles) * LANES, LANES), width)],
                sems.at[at_slot, part],
            )
            for part in range(3)
        ]

    @pl.when(step == 0)
    def _():
        table[...] = g_ref[...].astype(F32)
        mixed[...] = jnp.zeros(mixed.shape, F32)

    @pl.when(step >= 2)
    def _():
        for copy in copies(step - 2, slot):
            copy.wait()

    lane = lax.broadcasted_iota(jnp.int32, (1, LANES), 1)
    owner = lane // GROUP
    flip = (
        lax.broadcasted_iota(jnp.int32, (LANES, LANES), 0)
        + lax.broadcasted_iota(jnp.int32, (LANES, LANES), 1)
        == LANES - 1
    ).astype(F32).astype(BF)
    upside = (
        lax.broadcasted_iota(jnp.int32, (ROWS, ROWS), 0) ^ (PIECE - 1)
        == lax.broadcasted_iota(jnp.int32, (ROWS, ROWS), 1)
    ).astype(F32).astype(BF)
    owners = [(owner == g).astype(F32).astype(BF) for g in range(groups)]
    owners = [jnp.concatenate([m, m], axis=1) for m in owners]

    for t in range(tiles):
        tile = first_tile + step * tiles + t
        cols = slice(t * LANES, (t + 1) * LANES)
        filters = table[tile, 24:32, :]
        skip = taps_of(table, tile * 3)[7:8]
        flipped = jnp.dot(filters.astype(BF), flip, preferred_element_type=F32)
        forward = toeplitz_rows(flipped, 1)
        backward = toeplitz_rows(filters, 0)
        product = prod[:, cols]
        gated = gate[:, cols]
        context = jnp.concatenate([prior[:, cols], product], axis=0)
        coming = jnp.concatenate([gated, ahead[:, cols]], axis=0)
        turned = jnp.dot(upside, product, preferred_element_type=F32).astype(BF)
        wave, prod_grad = [], []
        lagged = None
        for pair in range(ROWS // (2 * PIECE)):
            low = 2 * PIECE * pair
            result = jnp.dot(forward, windows(context, pair), preferred_element_type=F32)
            wave += [picked(result[:, :LANES], owner), picked(result[:, LANES:], owner)]
            seen = windows(coming, pair)
            result = jnp.dot(backward, seen, preferred_element_type=F32)
            prod_grad += [picked(result[:, :LANES], owner), picked(result[:, LANES:], owner)]
            own = jnp.concatenate([turned[low : low + PIECE], turned[low + PIECE : low + 2 * PIECE]], axis=1)
            masked = jnp.concatenate([own * m for m in owners], axis=0)
            term = lax.dot_general(masked, seen, (((1,), (1,)), ((), ())), preferred_element_type=F32)
            lagged = term if lagged is None else lagged + term
        product = product.astype(F32)
        gated = gated.astype(F32)
        wave = jnp.concatenate(wave, axis=0) + skip * product
        prod_grad = jnp.concatenate(prod_grad, axis=0) + skip * gated
        corr[:, :SPAN] = lagged
        for g in range(groups):
            skewed = pltpu.roll(
                corr[g * PIECE : (g + 1) * PIECE, :], 2 * LANES - PIECE + 1, 1, stride=1, stride_axis=0
            )
            long_ref[t, g : g + 1, :] = jnp.sum(skewed[:, :LANES], axis=0, keepdims=True)
        long_ref[t, 8:9, :] = jnp.sum(gated * product, axis=0, keepdims=True)
        long_ref[t, 9:16, :] = jnp.zeros((7, LANES), F32)
        mixed[0, 8 : 8 + ROWS, :] = cot[0, :, cols].astype(F32) * wave
        mixed[1, 8 : 8 + ROWS, :] = prod_grad * val[:, cols].astype(F32)
        mixed[2, 8 : 8 + ROWS, :] = prod_grad * key[:, cols].astype(F32)
        heads = []
        for part, (source, halo) in enumerate(((sq, hq), (sk, hk), (sv, hv))):
            taps = taps_of(table, tile + part * count)
            feature = mixed.at[part]
            heads.append(feature[8:16, :])
            early = halo[:, cols].astype(F32)[8:16]
            values = source[0, :, cols].astype(F32)
            running = None
            sums = []
            for lag in range(SHORT):
                shifted = feature[8 + lag : 8 + lag + ROWS, :]
                term = taps[lag : lag + 1] * shifted
                running = term if running is None else running + term
                terms = shifted * values
                total = feature[lag : lag + 8, :] * early
                for r in range(ROWS // 8):
                    total = total + terms[r * 8 : (r + 1) * 8]
                sums.append(jnp.sum(total, axis=0, keepdims=True))
            sums.append(jnp.zeros((1, LANES), F32))
            short_ref[part, t, :, :] = jnp.concatenate(sums, axis=0)
            held[slot, part, :, cols] = running.astype(BF)
            tail_ref[part, :, cols] = running[ROWS - 16 :]
        head_ref[0, t * 24 : (t + 1) * 24, :] = jnp.concatenate(heads, axis=0).astype(BF)

    for copy in copies(step, slot):
        copy.start()

    @pl.when(step == steps - 1)
    def _():
        for copy in copies(step, slot):
            copy.wait()

    @pl.when(jnp.logical_and(step == steps - 1, step >= 1))
    def _():
        for copy in copies(step - 1, 1 - slot):
            copy.wait()


def back(first, width, gathered, streams, before, grad_out, made, prior, ahead, grads):
    count = grad_out.shape[2] // LANES
    step_width = min(width, 512)
    steps = width // step_width
    tiles = step_width // LANES
    blocks = grad_out.shape[2] // step_width
    lead = first // step_width
    product, gate, key, value = made

    def stream(part):
        return pl.BlockSpec((1, ROWS, step_width), lambda i: (0, 0, part * blocks + lead + i))

    def halo(part):
        return pl.BlockSpec((16, step_width), lambda i: (0, part * blocks + lead + i))

    local = pl.BlockSpec((ROWS, step_width), lambda i: (0, i))
    chained = grads is not None
    operands = [gathered, streams, streams, streams, before, before, before, grad_out, product, prior, gate, ahead, key, value]
    in_specs = (
        [pl.BlockSpec(gathered.shape, lambda i: (0, 0, 0))]
        + [stream(part) for part in range(3)]
        + [halo(part) for part in range(3)]
        + [pl.BlockSpec((1, ROWS, step_width), lambda i: (0, 0, lead + i))]
        + [local] * 6
    )
    if chained:
        operands.append(grads)
        in_specs.append(anywhere())
    return pl.pallas_call(
        functools.partial(back_kernel, first // LANES, tiles, count, chained),
        grid=(steps,),
        out_shape=(
            jax.ShapeDtypeStruct(streams.shape, BF),
            jax.ShapeDtypeStruct((3, 16, width), F32),
            jax.ShapeDtypeStruct((steps, tiles * 24, LANES), BF),
            jax.ShapeDtypeStruct((3, width // LANES, 8, LANES), F32),
            jax.ShapeDtypeStruct((width // LANES, 16, LANES), F32),
        ),
        in_specs=in_specs,
        out_specs=(
            anywhere(),
            pl.BlockSpec((3, 16, step_width), lambda i: (0, 0, i)),
            pl.BlockSpec((1, tiles * 24, LANES), lambda i: (i, 0, 0)),
            pl.BlockSpec((3, tiles, 8, LANES), lambda i: (0, i, 0, 0)),
            pl.BlockSpec((tiles, 16, LANES), lambda i: (i, 0, 0)),
        ),
        scratch_shapes=[
            pltpu.VMEM(gathered.shape, F32),
            pltpu.VMEM((3, 8 + ROWS + 8, LANES), F32),
            pltpu.VMEM((LANES, 2 * LANES), F32),
            pltpu.VMEM((2, 3, ROWS, step_width), BF),
            pltpu.SemaphoreType.DMA((2, 3)),
        ],
        input_output_aliases={len(operands) - 1: 0} if chained else {},
        compiler_params=params(48),
        cost_estimate=pl.CostEstimate(
            flops=600 * 3 * ROWS * width, bytes_accessed=24 * ROWS * width, transcendentals=0
        ),
        name="back",
    )(*operands)


def finish_kernel(chunks, count, g_ref, *refs):
    tails = refs[:chunks]
    heads = refs[chunks : 2 * chunks]
    _, gs_ref, strip, sem = refs[2 * chunks :]
    per_chunk = count // chunks
    for c in range(chunks):
        steps = heads[c].shape[0]
        per_step = heads[c].shape[1] // 24
        for step in range(steps):
            block = heads[c][step].astype(F32)
            for t in range(per_step):
                here = step * per_step + t
                for part in range(3):
                    tile = part * count + c * per_chunk + here
                    low = 24 * t + 8 * part
                    taps = g_ref[tile // 3].astype(F32)[tile % 3 * 8 : tile % 3 * 8 + 8]
                    after = jnp.concatenate([jnp.zeros((8, LANES), F32), block[low : low + 8]], axis=0)
                    tail = tails[c][part, :, here * LANES : (here + 1) * LANES]
                    last = tail[8:16]
                    for lag in range(1, SHORT):
                        last = last + taps[lag : lag + 1] * after[lag : lag + 8]
                    strip[:, tile * LANES : (tile + 1) * LANES] = jnp.concatenate([tail[0:8], last], axis=0).astype(BF)
    copy = pltpu.make_async_copy(strip, gs_ref.at[0, pl.ds(ROWS - 16, 16), :], sem)
    copy.start()
    copy.wait()


def finish(gathered, tails, heads, grads):
    chunks = len(tails)
    count = grads.shape[2] // LANES // 3
    return pl.pallas_call(
        functools.partial(finish_kernel, chunks, count),
        out_shape=jax.ShapeDtypeStruct(grads.shape, BF),
        in_specs=[whole()] * (1 + 2 * chunks) + [anywhere()],
        out_specs=anywhere(),
        scratch_shapes=[pltpu.VMEM((16, grads.shape[2]), BF), pltpu.SemaphoreType.DMA],
        input_output_aliases={1 + 2 * chunks: 0},
        compiler_params=params(32),
        cost_estimate=pl.CostEstimate(flops=10000000, bytes_accessed=2000000, transcendentals=0),
        name="finish",
    )(gathered, *tails, *heads, grads)


def bundle_kernel(chunks, shards, *refs):
    shorts, longs, out_ref = refs[:chunks], refs[chunks : 2 * chunks], refs[2 * chunks]
    per_chunk = shards // chunks

    def short(tile):
        part, here = divmod(tile, shards)
        return shorts[here // per_chunk][part, here % per_chunk]

    for d in range(shards):
        long = longs[d // per_chunk][d % per_chunk]
        rows = [short(3 * d)[0:7], long[8:9], short(3 * d + 1), short(3 * d + 2), long[0:8]]
        out_ref[d] = jnp.concatenate(rows, axis=0).astype(BF)


def bundle(shorts, longs, shards):
    chunks = len(shorts)
    return pl.pallas_call(
        functools.partial(bundle_kernel, chunks, shards),
        out_shape=jax.ShapeDtypeStruct((shards, 32, LANES), BF),
        in_specs=[whole()] * (2 * chunks),
        out_specs=whole(),
        compiler_params=params(16),
        name="bundle",
    )(*shorts, *longs)


def total_kernel(parts_ref, out_ref):
    out_ref[...] = jnp.sum(parts_ref[...].astype(F32), axis=0)


def total(parts):
    return pl.pallas_call(
        total_kernel,
        out_shape=jax.ShapeDtypeStruct(parts.shape[1:], F32),
        in_specs=[whole()],
        out_specs=whole(),
        compiler_params=params(16),
        name="total",
    )(parts)


def spread_kernel(scale, place_ref, *refs):
    parts, (short_ref, long_ref, skip_ref, held) = refs[:-4], refs[-4:]
    count = len(parts)
    for i in range(count):
        held[i] = parts[i][...]
    summed = None
    for device in range(count):
        part = held[lax.rem(place_ref[0] - device + count, count)]
        summed = part if summed is None else summed + part
    summed = summed * scale
    for part in range(3):
        short_ref[:, part * LANES : (part + 1) * LANES] = summed[8 * part : 8 * part + SHORT]
    long_ref[...] = summed[24:32]
    skip_ref[...] = summed[7:8]


def spread(place, parts, scale):
    return pl.pallas_call(
        functools.partial(spread_kernel, scale),
        out_shape=(
            jax.ShapeDtypeStruct((SHORT, 3 * LANES), F32),
            jax.ShapeDtypeStruct((8, LANES), F32),
            jax.ShapeDtypeStruct((1, LANES), F32),
        ),
        in_specs=[pl.BlockSpec(memory_space=pltpu.SMEM)] + [whole()] * len(parts),
        out_specs=(whole(),) * 3,
        scratch_shapes=[pltpu.VMEM((len(parts), 32, LANES), F32)],
        compiler_params=params(16),
        name="spread",
    )(place, *parts)


def passed_along(block, axis, distance):
    devices = range(lax.axis_size(axis))
    route = [(i - distance, i) for i in devices if i - distance in devices]
    return lax.ppermute(block, axis, route)


CHUNKS = 4


def local(streams, short_filter, long_filter, skip, grad_out):
    shards = lax.axis_size("dp")
    ring = lax.axis_size("seq")
    width = grad_out.shape[2] // CHUNKS
    payload, tail_rows = pack(short_filter, long_filter, skip, streams, shards)
    before = passed_along(tail_rows, "seq", 1)
    gathered = lax.all_to_all(payload, "dp", 0, 0, tiled=True)
    made = [gates(c * width, width, gathered, streams, before, grad_out) for c in range(CHUNKS)]
    prior = [passed_along(m[0], "seq", 1) for m in made]
    ahead = [passed_along(m[1], "seq", -1) for m in made]
    grads = None
    tails, heads, shorts, longs = [], [], [], []
    for c in range(CHUNKS):
        grads, tail, head, short, long = back(
            c * width, width, gathered, streams, before, grad_out, made[c], prior[c], ahead[c], grads
        )
        tails.append(tail)
        heads.append(head)
        shorts.append(short)
        longs.append(long)
    after = [passed_along(head, "seq", -1) for head in heads]
    grads = finish(gathered, tails, after, grads)
    own = total(lax.all_to_all(bundle(shorts, longs, shards), "dp", 0, 0, tiled=True))
    parts = [own]
    for distance in range(1, ring):
        parts.append(lax.ppermute(own, "seq", [(i, (i + distance) % ring) for i in range(ring)]))
    scale = 1.0 / math.sqrt(shards * ring * streams.shape[1])
    place = lax.axis_index("seq").astype(jnp.int32)[None]
    grad_short, grad_long, grad_skip = spread(place, parts, scale)
    return grads, grad_short, grad_long, grad_skip[0]


def solution(mesh):
    placed = (P("dp", "seq", None), P(None, "dp"), P("dp", None), P("dp"), P("dp", "seq", None))
    return jax.shard_map(
        local,
        mesh=mesh,
        in_specs=placed,
        out_specs=(P("dp", "seq", None), P(None, "dp"), P("dp", None), P("dp")),
        check_vma=False,
    )
```

```python
import functools
import math

import jax
import jax.numpy as jnp
from jax import lax
from jax.experimental import pallas as pl
from jax.experimental.pallas import tpu as pltpu
from jax.sharding import PartitionSpec as P

LANES = 128
GROUP = 16
SHORT = 7
ROWS = 128
FULL = 20
STEP = 512
PIECE = 16
SPAN = PIECE + 128
BF = jnp.bfloat16
F32 = jnp.float32


def params(mib):
    return pltpu.CompilerParams(vmem_limit_bytes=mib * 1024 * 1024)


def whole():
    return pl.BlockSpec(memory_space=pltpu.VMEM)


def in_hbm(array):
    return pltpu.with_memory_space_constraint(array, pltpu.HBM)


def anywhere():
    return pl.BlockSpec(memory_space=pl.ANY)


def pack_kernel(short_ref, long_ref, skip_ref, streams_ref, out_ref, tail_ref):
    tail_ref[...] = streams_ref[0]
    short = short_ref[...].astype(F32)
    skip = skip_ref[...].astype(F32)
    nothing = jnp.zeros((1, LANES), F32)
    rows = []
    for part in range(3):
        rows.append(short[:, part * LANES : (part + 1) * LANES])
        rows.append(skip if part == 0 else nothing)
    packed = jnp.concatenate(rows + [long_ref[...].astype(F32)], axis=0).astype(BF)
    out_ref[...] = jnp.broadcast_to(packed[None], out_ref.shape)


def pack(short_filter, long_filter, skip, streams, shards):
    return pl.pallas_call(
        pack_kernel,
        out_shape=(
            jax.ShapeDtypeStruct((shards, 32, LANES), BF),
            jax.ShapeDtypeStruct((16, streams.shape[2]), BF),
        ),
        in_specs=[
            pl.BlockSpec(short_filter.shape, lambda i: (0, 0)),
            pl.BlockSpec(long_filter.shape, lambda i: (0, 0)),
            pl.BlockSpec((1, LANES), lambda i: (0, 0)),
            pl.BlockSpec((1, 16, streams.shape[2]), lambda i: (0, ROWS // 16 - 1, 0)),
        ],
        out_specs=(
            pl.BlockSpec((shards, 32, LANES), lambda i: (0, 0, 0)),
            pl.BlockSpec((16, streams.shape[2]), lambda i: (0, 0)),
        ),
        grid=(1,),
        compiler_params=params(20),
        name="pack",
    )(*(in_hbm(x) for x in (short_filter, long_filter, skip[None], streams)))


def taps_of(table, tile):
    return table[tile // 3, pl.ds(pl.multiple_of(tile % 3 * 8, 8), 8), :]


def mixture(slot, halo, source, taps):
    slot[0:8, :] = halo
    slot[8 : 8 + ROWS, :] = source.astype(F32)
    running = taps[0:1] * slot[8 : 8 + ROWS, :]
    for lag in range(1, SHORT):
        running = running + taps[lag : lag + 1] * slot[8 - lag : 8 - lag + ROWS, :]
    return running


def gates_kernel(first_tile, count, g_ref, sq, sk, sv, hq, hk, hv, cot, prod, gate, key, val, table, ext):
    step = pl.program_id(0)
    tiles = STEP // LANES

    @pl.when(step == 0)
    def _():
        table[...] = g_ref[...].astype(F32)

    for t in range(tiles):
        tile = first_tile + step * tiles + t
        cols = slice(t * LANES, (t + 1) * LANES)
        mixed = []
        for part, (source, halo) in enumerate(((sq, hq), (sk, hk), (sv, hv))):
            taps = taps_of(table, tile + part * count)
            mixed.append(mixture(ext.at[t, part], halo[:, cols].astype(F32)[8:16], source[0, :, cols], taps))
        prod[:, cols] = (mixed[1] * mixed[2]).astype(BF)
        gate[:, cols] = (cot[0, :, cols].astype(F32) * mixed[0]).astype(BF)
        key[:, cols] = mixed[1].astype(BF)
        val[:, cols] = mixed[2].astype(BF)


def stream_specs(lead, blocks):
    def stream(part):
        return pl.BlockSpec((1, ROWS, STEP), lambda i: (0, 0, part * blocks + lead + i))

    def halo(part):
        return pl.BlockSpec((16, STEP), lambda i: (0, part * blocks + lead + i))

    return (
        [stream(part) for part in range(3)]
        + [halo(part) for part in range(3)]
        + [pl.BlockSpec((1, ROWS, STEP), lambda i: (0, 0, lead + i))]
    )


def gates(first, width, gathered, streams, before, grad_out):
    count = grad_out.shape[2] // LANES
    steps = width // STEP
    lead = first // STEP
    out = jax.ShapeDtypeStruct((ROWS, width), BF)
    out_spec = pl.BlockSpec((ROWS, STEP), lambda i: (0, i))
    return pl.pallas_call(
        functools.partial(gates_kernel, first // LANES, count),
        grid=(steps,),
        out_shape=(out,) * 4,
        in_specs=[pl.BlockSpec(gathered.shape, lambda i: (0, 0, 0))]
        + stream_specs(lead, grad_out.shape[2] // STEP),
        out_specs=(out_spec,) * 4,
        scratch_shapes=[
            pltpu.VMEM(gathered.shape, F32),
            pltpu.VMEM((STEP // LANES, 3, 8 + ROWS, LANES), F32),
        ],
        compiler_params=params(FULL),
        cost_estimate=pl.CostEstimate(
            flops=60 * 3 * ROWS * width, bytes_accessed=16 * ROWS * width, transcendentals=0
        ),
        name="gates",
    )(gathered, streams, streams, streams, before, before, before, grad_out)


def windows(block, pair):
    low = 2 * PIECE * pair
    return jnp.concatenate(
        [block[low : low + SPAN], block[low + PIECE : low + PIECE + SPAN]], axis=1
    )


def picked(result, owner):
    out = result[0:PIECE]
    for g in range(1, LANES // GROUP):
        out = jnp.where(owner == g, result[g * PIECE : (g + 1) * PIECE], out)
    return out


def toeplitz_rows(filters, shift):
    pieces = []
    for g in range(LANES // GROUP):
        line = jnp.concatenate([filters[g : g + 1], jnp.zeros((1, LANES), F32)], axis=1)
        line = jnp.broadcast_to(line, (PIECE, 2 * LANES))
        pieces.append(pltpu.roll(line, shift, 1, stride=1, stride_axis=0))
    return jnp.concatenate(pieces, axis=0).astype(BF)


def bands_kernel(tiles, g_ref, forward_ref, backward_ref):
    step = pl.program_id(0)
    flip = (
        lax.broadcasted_iota(jnp.int32, (LANES, LANES), 0)
        + lax.broadcasted_iota(jnp.int32, (LANES, LANES), 1)
        == LANES - 1
    ).astype(F32).astype(BF)
    for t in range(tiles):
        filters = g_ref[step * tiles + t].astype(F32)[24:32]
        flipped = jnp.dot(filters.astype(BF), flip, preferred_element_type=F32)
        forward_ref[t] = toeplitz_rows(flipped, 1)
        backward_ref[t] = toeplitz_rows(filters, 0)


def bands(gathered):
    shards = gathered.shape[0]
    tiles = 8
    out = jax.ShapeDtypeStruct((shards, LANES, 2 * LANES), BF)
    spec = pl.BlockSpec((tiles, LANES, 2 * LANES), lambda i: (i, 0, 0))
    return pl.pallas_call(
        functools.partial(bands_kernel, tiles),
        grid=(shards // tiles,),
        out_shape=(out, out),
        in_specs=[pl.BlockSpec(gathered.shape, lambda i: (0, 0, 0))],
        out_specs=(spec, spec),
        compiler_params=params(FULL),
        cost_estimate=pl.CostEstimate(flops=400000000, bytes_accessed=4000000, transcendentals=0),
        name="bands",
    )(gathered)


def back_kernel(
    first_tile, tiles, count, chained, g_ref, sq, sk, sv, hq, hk, hv, cot, prod, prior, gate, ahead, key, val, fw, bw, *rest
):
    if chained:
        rest = rest[5:]
    gs_ref, tail_ref, head_ref, short_ref, long_ref, table, ext, mixed, corr, held, sems = rest
    step = pl.program_id(0)
    steps = pl.num_programs(0)
    slot = lax.rem(step, 2)
    groups = LANES // GROUP

    def copies(at_step, at_slot):
        place = first_tile + at_step * tiles
        return [
            pltpu.make_async_copy(
                held.at[at_slot, part],
                gs_ref.at[0, :, pl.ds(pl.multiple_of((part * count + place) * LANES, STEP), STEP)],
                sems.at[at_slot, part],
            )
            for part in range(3)
        ]

    @pl.when(step >= 2)
    def _():
        for copy in copies(step - 2, slot):
            copy.wait()

    @pl.when(step == 0)
    def _():
        table[...] = g_ref[...].astype(F32)

    lane = lax.broadcasted_iota(jnp.int32, (1, LANES), 1)
    owner = lane // GROUP
    upside = (
        lax.broadcasted_iota(jnp.int32, (ROWS, ROWS), 0) ^ (PIECE - 1)
        == lax.broadcasted_iota(jnp.int32, (ROWS, ROWS), 1)
    ).astype(F32).astype(BF)
    owners = [(owner == g).astype(F32).astype(BF) for g in range(groups)]
    owners = [jnp.concatenate([m, m], axis=1) for m in owners]

    for t in range(tiles):
        tile = first_tile + step * tiles + t
        cols = slice(t * LANES, (t + 1) * LANES)
        skip = taps_of(table, tile * 3)[7:8]
        forward = fw[t, :, :SPAN]
        backward = bw[t, :, :SPAN]
        product = prod[:, cols]
        gated = gate[:, cols]
        context = jnp.concatenate([prior[:, cols], product], axis=0)
        coming = jnp.concatenate([gated, ahead[:, cols]], axis=0)
        turned = jnp.dot(upside, product, preferred_element_type=F32).astype(BF)
        wave, prod_grad = [], []
        lagged = None
        for pair in range(ROWS // (2 * PIECE)):
            low = 2 * PIECE * pair
            result = jnp.dot(forward, windows(context, pair), preferred_element_type=F32)
            wave += [picked(result[:, :LANES], owner), picked(result[:, LANES:], owner)]
            seen = windows(coming, pair)
            result = jnp.dot(backward, seen, preferred_element_type=F32)
            prod_grad += [picked(result[:, :LANES], owner), picked(result[:, LANES:], owner)]
            own = jnp.concatenate([turned[low : low + PIECE], turned[low + PIECE : low + 2 * PIECE]], axis=1)
            masked = jnp.concatenate([own * m for m in owners], axis=0)
            term = lax.dot_general(masked, seen, (((1,), (1,)), ((), ())), preferred_element_type=F32)
            lagged = term if lagged is None else lagged + term
        product = product.astype(F32)
        gated = gated.astype(F32)
        wave = jnp.concatenate(wave, axis=0) + skip * product
        prod_grad = jnp.concatenate(prod_grad, axis=0) + skip * gated
        corr[t, :, :SPAN] = lagged
        for g in range(groups):
            skewed = pltpu.roll(
                corr[t, g * PIECE : (g + 1) * PIECE, :], 2 * LANES - PIECE + 1, 1, stride=1, stride_axis=0
            )
            long_ref[t, g : g + 1, :] = jnp.sum(skewed[:, :LANES], axis=0, keepdims=True)
        long_ref[t, 8:9, :] = jnp.sum(gated * product, axis=0, keepdims=True)
        long_ref[t, 9:16, :] = jnp.zeros((7, LANES), F32)
        features = (
            cot[0, :, cols].astype(F32) * wave,
            prod_grad * val[:, cols].astype(F32),
            prod_grad * key[:, cols].astype(F32),
        )
        for part, (source, halo) in enumerate(((sq, hq), (sk, hk), (sv, hv))):
            taps = taps_of(table, tile + part * count)
            feature = features[part]
            shifted = mixed.at[t, part]
            shifted[0:ROWS, :] = feature
            shifted[ROWS : ROWS + 8, :] = jnp.zeros((8, LANES), F32)
            head_ref[part, :, cols] = feature[0:8].astype(BF)
            early = ext.at[t, part]
            early[0:8, :] = halo[:, cols].astype(F32)[8:16]
            early[8 : 8 + ROWS, :] = source[0, :, cols].astype(F32)
            sums = []
            running = taps[0:1] * feature
            for lag in range(SHORT):
                terms = feature * early[8 - lag : 8 - lag + ROWS, :]
                total = terms[0:8]
                for r in range(1, ROWS // 8):
                    total = total + terms[r * 8 : (r + 1) * 8]
                sums.append(jnp.sum(total, axis=0, keepdims=True))
                if lag > 0:
                    running = running + taps[lag : lag + 1] * shifted[lag : lag + ROWS, :]
            sums.append(jnp.zeros((1, LANES), F32))
            short_ref[part, t, :, :] = jnp.concatenate(sums, axis=0)
            held[slot, part, :, cols] = running.astype(BF)
            tail_ref[part, t] = running[ROWS - 16 :]

    for copy in copies(step, slot):
        copy.start()

    @pl.when(step == steps - 1)
    def _():
        for copy in copies(step, slot):
            copy.wait()

    @pl.when(jnp.logical_and(step == steps - 1, step >= 1))
    def _():
        for copy in copies(step - 1, 1 - slot):
            copy.wait()


def back(first, width, gathered, streams, before, grad_out, made, prior, ahead, filters, chain):
    count = grad_out.shape[2] // LANES
    steps = width // STEP
    tiles = STEP // LANES
    lead = first // STEP
    product, gate, key, value = made

    local = pl.BlockSpec((ROWS, STEP), lambda i: (0, i))
    band = pl.BlockSpec((tiles, LANES, 2 * LANES), lambda i: (lead + i, 0, 0))
    operands = [gathered, streams, streams, streams, before, before, before, grad_out]
    operands += [product, prior, gate, ahead, key, value, *filters]
    in_specs = (
        [pl.BlockSpec(gathered.shape, lambda i: (0, 0, 0))]
        + stream_specs(lead, grad_out.shape[2] // STEP)
        + [local] * 6
        + [band] * 2
    )
    aliases = {}
    if chain is not None:
        aliases = {len(operands) + i: i for i in range(5)}
        operands += chain
        in_specs += [anywhere()] * 5
    return pl.pallas_call(
        functools.partial(back_kernel, first // LANES, tiles, count, chain is not None),
        grid=(steps,),
        out_shape=(
            jax.ShapeDtypeStruct(streams.shape, BF),
            jax.ShapeDtypeStruct((3, count, 16, LANES), F32),
            jax.ShapeDtypeStruct((3, 8, grad_out.shape[2]), BF),
            jax.ShapeDtypeStruct((3, count, 8, LANES), F32),
            jax.ShapeDtypeStruct((count, 16, LANES), F32),
        ),
        in_specs=in_specs,
        out_specs=(
            anywhere(),
            pl.BlockSpec((3, tiles, 16, LANES), lambda i: (0, lead + i, 0, 0)),
            pl.BlockSpec((3, 8, STEP), lambda i: (0, 0, lead + i)),
            pl.BlockSpec((3, tiles, 8, LANES), lambda i: (0, lead + i, 0, 0)),
            pl.BlockSpec((tiles, 16, LANES), lambda i: (lead + i, 0, 0)),
        ),
        scratch_shapes=[
            pltpu.VMEM(gathered.shape, F32),
            pltpu.VMEM((tiles, 3, 8 + ROWS, LANES), F32),
            pltpu.VMEM((tiles, 3, ROWS + 8, LANES), F32),
            pltpu.VMEM((tiles, LANES, 2 * LANES), F32),
            pltpu.VMEM((2, 3, ROWS, STEP), BF),
            pltpu.SemaphoreType.DMA((2, 3)),
        ],
        input_output_aliases=aliases,
        compiler_params=params(FULL),
        cost_estimate=pl.CostEstimate(
            flops=600 * 3 * ROWS * width, bytes_accessed=24 * ROWS * width, transcendentals=0
        ),
        name="back",
    )(*operands)


def finish_kernel(count, g_ref, after_ref, tail_ref, _, gs_ref, strip, sem):
    for part in range(3):
        for here in range(count):
            tile = part * count + here
            taps = g_ref[tile // 3].astype(F32)[tile % 3 * 8 : tile % 3 * 8 + 8]
            after = after_ref[part, :, here * LANES : (here + 1) * LANES].astype(F32)
            after = jnp.concatenate([jnp.zeros((8, LANES), F32), after], axis=0)
            tail = tail_ref[part, here]
            last = tail[8:16]
            for lag in range(1, SHORT):
                last = last + taps[lag : lag + 1] * after[lag : lag + 8]
            strip[:, tile * LANES : (tile + 1) * LANES] = jnp.concatenate([tail[0:8], last], axis=0).astype(BF)
    copy = pltpu.make_async_copy(strip, gs_ref.at[0, pl.ds(ROWS - 16, 16), :], sem)
    copy.start()
    copy.wait()


def finish(gathered, after, tails, grads):
    return pl.pallas_call(
        functools.partial(finish_kernel, tails.shape[1]),
        out_shape=jax.ShapeDtypeStruct(grads.shape, BF),
        in_specs=[whole()] * 3 + [anywhere()],
        out_specs=anywhere(),
        scratch_shapes=[pltpu.VMEM((16, grads.shape[2]), BF), pltpu.SemaphoreType.DMA],
        input_output_aliases={3: 0},
        compiler_params=params(FULL),
        cost_estimate=pl.CostEstimate(flops=10000000, bytes_accessed=2000000, transcendentals=0),
        name="finish",
    )(gathered, after, tails, grads)


def bundle_kernel(shards, short_ref, long_ref, out_ref):
    def short(tile):
        return short_ref[tile // shards, tile % shards]

    for d in range(shards):
        long = long_ref[d]
        rows = [short(3 * d)[0:7], long[8:9], short(3 * d + 1), short(3 * d + 2), long[0:8]]
        out_ref[d] = jnp.concatenate(rows, axis=0).astype(BF)


def bundle(short, long, shards):
    return pl.pallas_call(
        functools.partial(bundle_kernel, shards),
        out_shape=jax.ShapeDtypeStruct((shards, 32, LANES), BF),
        in_specs=[whole()] * 2,
        out_specs=whole(),
        compiler_params=params(16),
        name="bundle",
    )(short, long)


def total_kernel(parts_ref, out_ref):
    out_ref[...] = jnp.broadcast_to(jnp.sum(parts_ref[...].astype(F32), axis=0).astype(BF)[None], out_ref.shape)


def total(parts, copies):
    return pl.pallas_call(
        total_kernel,
        out_shape=jax.ShapeDtypeStruct((copies,) + parts.shape[1:], BF),
        in_specs=[whole()],
        out_specs=whole(),
        compiler_params=params(16),
        name="total",
    )(parts)


def spread_kernel(scale, parts_ref, short_ref, long_ref, skip_ref):
    summed = jnp.sum(parts_ref[...].astype(F32), axis=0) * scale
    for part in range(3):
        short_ref[:, part * LANES : (part + 1) * LANES] = summed[8 * part : 8 * part + SHORT]
    long_ref[...] = summed[24:32]
    skip_ref[...] = summed[7:8]


def spread(parts, scale):
    return pl.pallas_call(
        functools.partial(spread_kernel, scale),
        out_shape=(
            jax.ShapeDtypeStruct((SHORT, 3 * LANES), F32),
            jax.ShapeDtypeStruct((8, LANES), F32),
            jax.ShapeDtypeStruct((1, LANES), F32),
        ),
        in_specs=[whole()],
        out_specs=(whole(),) * 3,
        compiler_params=params(16),
        name="spread",
    )(parts)


def passed_along(block, axis, distance):
    devices = range(lax.axis_size(axis))
    route = [(i - distance, i) for i in devices if i - distance in devices]
    return lax.ppermute(block, axis, route)


CHUNKS = (2560, 1536)


def local(streams, short_filter, long_filter, skip, grad_out):
    shards = lax.axis_size("dp")
    ring = lax.axis_size("seq")
    payload, tail_rows = pack(short_filter, long_filter, skip, streams, shards)
    before = passed_along(tail_rows, "seq", 1)
    gathered = lax.all_to_all(payload, "dp", 0, 0, tiled=True)
    work = []
    first = 0
    for width in CHUNKS:
        made = gates(first, width, gathered, streams, before, grad_out)
        work.append((first, width, made, passed_along(made[0], "seq", 1), passed_along(made[1], "seq", -1)))
        first += width
    filters = bands(gathered)
    chain = None
    for first, width, made, prior, ahead in work:
        chain = back(first, width, gathered, streams, before, grad_out, made, prior, ahead, filters, chain)
    grads, tails, head, short, long = chain
    after = passed_along(head, "seq", -1)
    parts = total(lax.all_to_all(bundle(short, long, shards), "dp", 0, 0, tiled=True), ring)
    parts = lax.all_to_all(parts, "seq", 0, 0, tiled=True)
    scale = 1.0 / math.sqrt(shards * ring * streams.shape[1])
    grad_short, grad_long, grad_skip = spread(parts, scale)
    grads = finish(gathered, after, tails, grads)
    return grads, grad_short, grad_long, grad_skip[0]


def solution(mesh):
    placed = (P("dp", "seq", None), P(None, "dp"), P("dp", None), P("dp"), P("dp", "seq", None))
    return jax.shard_map(
        local,
        mesh=mesh,
        in_specs=placed,
        out_specs=(P("dp", "seq", None), P(None, "dp"), P("dp", None), P("dp")),
        check_vma=False,
    )
```

```python
import functools
import math

import jax
import jax.numpy as jnp
from jax import lax
from jax.experimental import pallas as pl
from jax.experimental.pallas import tpu as pltpu
from jax.sharding import PartitionSpec as P

LANES = 128
GROUP = 16
SHORT = 7
ROWS = 128
FULL = 6
UNROLL = 4
PIECE = 16
SPAN = PIECE + 128
BF = jnp.bfloat16
F32 = jnp.float32


def params(mib):
    return pltpu.CompilerParams(vmem_limit_bytes=mib * 1024 * 1024)


def whole():
    return pl.BlockSpec(memory_space=pltpu.VMEM)


def in_hbm(array):
    return pltpu.with_memory_space_constraint(array, pltpu.HBM)


def anywhere():
    return pl.BlockSpec(memory_space=pl.ANY)


def pack_kernel(short_ref, long_ref, skip_ref, streams_ref, out_ref, tail_ref):
    tail_ref[...] = streams_ref[0]
    short = short_ref[...].astype(F32)
    skip = skip_ref[...].astype(F32)
    nothing = jnp.zeros((1, LANES), F32)
    rows = []
    for part in range(3):
        rows.append(short[:, part * LANES : (part + 1) * LANES])
        rows.append(skip if part == 0 else nothing)
    packed = jnp.concatenate(rows + [long_ref[...].astype(F32)], axis=0).astype(BF)
    out_ref[...] = jnp.broadcast_to(packed[None], out_ref.shape)


def pack(short_filter, long_filter, skip, streams, shards):
    return pl.pallas_call(
        pack_kernel,
        out_shape=(
            jax.ShapeDtypeStruct((shards, 32, LANES), BF),
            jax.ShapeDtypeStruct((16, streams.shape[2]), BF),
        ),
        in_specs=[
            pl.BlockSpec(short_filter.shape, lambda i: (0, 0)),
            pl.BlockSpec(long_filter.shape, lambda i: (0, 0)),
            pl.BlockSpec((1, LANES), lambda i: (0, 0)),
            pl.BlockSpec((1, 16, streams.shape[2]), lambda i: (0, ROWS // 16 - 1, 0)),
        ],
        out_specs=(
            pl.BlockSpec((shards, 32, LANES), lambda i: (0, 0, 0)),
            pl.BlockSpec((16, streams.shape[2]), lambda i: (0, 0)),
        ),
        grid=(1,),
        compiler_params=params(FULL),
        name="pack",
    )(*(in_hbm(x) for x in (short_filter, long_filter, skip[None], streams)))


def taps_of(table, tile):
    return table[tile // 3, pl.ds(pl.multiple_of(tile % 3 * 8, 8), 8), :]


def lanes_of(tile):
    start = tile * LANES
    return pl.ds(start if isinstance(start, int) else pl.multiple_of(start, LANES), LANES)


def mixture(slot, halo, source, taps):
    slot[0:8, :] = halo
    slot[8 : 8 + ROWS, :] = source.astype(F32)
    running = taps[0:1] * slot[8 : 8 + ROWS, :]
    for lag in range(1, SHORT):
        running = running + taps[lag : lag + 1] * slot[8 - lag : 8 - lag + ROWS, :]
    return running


def gates_kernel(first, lead, count, g_ref, streams, before, cot, *rest):
    if lead:
        prod, gate, key, val, table, ext = rest
        table[...] = g_ref[...].astype(F32)
    else:
        prod, gate, key, val, ext = rest
        table = g_ref

    def some(step, _):
        for t in range(UNROLL):
            here = step * UNROLL + t
            tile = first // LANES + here
            cols = lanes_of(here)
            mixed = []
            for part in range(3):
                whence = lanes_of(tile + part * count)
                taps = taps_of(table, tile + part * count)
                halo = before[:, whence].astype(F32)[8:16]
                mixed.append(mixture(ext.at[t, part], halo, streams[0, :, whence], taps))
            prod[:, cols] = (mixed[1] * mixed[2]).astype(BF)
            gate[:, cols] = (cot[0, :, lanes_of(tile)].astype(F32) * mixed[0]).astype(BF)
            key[:, cols] = mixed[1].astype(BF)
            val[:, cols] = mixed[2].astype(BF)
        return 0

    for step in range(prod.shape[1] // LANES // UNROLL):
        some(step, 0)


def gates(first, width, table, streams, before, grad_out, lead):
    count = grad_out.shape[2] // LANES
    outs = [jax.ShapeDtypeStruct((ROWS, width), BF)] * 4
    if lead:
        outs.append(jax.ShapeDtypeStruct(table.shape, F32))
    return pl.pallas_call(
        functools.partial(gates_kernel, first, lead, count),
        out_shape=tuple(outs),
        in_specs=[whole()] * 4,
        out_specs=(whole(),) * len(outs),
        scratch_shapes=[pltpu.VMEM((UNROLL, 3, 8 + ROWS, LANES), F32)],
        compiler_params=params(FULL),
        cost_estimate=pl.CostEstimate(
            flops=60 * 3 * ROWS * width, bytes_accessed=16 * ROWS * width, transcendentals=0
        ),
        name="gates",
    )(table, streams, before, grad_out)


def windows(block, pair):
    low = 2 * PIECE * pair
    return jnp.concatenate(
        [block[low : low + SPAN], block[low + PIECE : low + PIECE + SPAN]], axis=1
    )


def picked(result, owner):
    out = result[0:PIECE]
    for g in range(1, LANES // GROUP):
        out = jnp.where(owner == g, result[g * PIECE : (g + 1) * PIECE], out)
    return out


def toeplitz_rows(filters, shift):
    pieces = []
    for g in range(LANES // GROUP):
        line = jnp.concatenate([filters[g : g + 1], jnp.zeros((1, LANES), F32)], axis=1)
        line = jnp.broadcast_to(line, (PIECE, 2 * LANES))
        pieces.append(pltpu.roll(line, shift, 1, stride=1, stride_axis=0))
    return jnp.concatenate(pieces, axis=0).astype(BF)


def bands_kernel(tiles, g_ref, forward_ref, backward_ref):
    step = pl.program_id(0)
    flip = (
        lax.broadcasted_iota(jnp.int32, (LANES, LANES), 0)
        + lax.broadcasted_iota(jnp.int32, (LANES, LANES), 1)
        == LANES - 1
    ).astype(F32).astype(BF)
    for t in range(tiles):
        filters = g_ref[step * tiles + t, 24:32, :]
        flipped = jnp.dot(filters.astype(BF), flip, preferred_element_type=F32)
        forward_ref[t] = toeplitz_rows(flipped, 1)
        backward_ref[t] = toeplitz_rows(filters, 0)


def bands(gathered):
    shards = gathered.shape[0]
    tiles = 8
    out = jax.ShapeDtypeStruct((shards, LANES, 2 * LANES), BF)
    spec = pl.BlockSpec((tiles, LANES, 2 * LANES), lambda i: (i, 0, 0))
    return pl.pallas_call(
        functools.partial(bands_kernel, tiles),
        grid=(shards // tiles,),
        out_shape=(out, out),
        in_specs=[pl.BlockSpec(gathered.shape, lambda i: (0, 0, 0))],
        out_specs=(spec, spec),
        compiler_params=params(FULL),
        cost_estimate=pl.CostEstimate(flops=400000000, bytes_accessed=4000000, transcendentals=0),
        name="bands",
    )(gathered)


def back_kernel(
    first, count, table, streams, before, cot, prod, gate, key, val, prior, ahead, fw, bw, *rest
):
    if first > 0:
        earlier, *rest = rest
    gs_ref, tail_ref, head_ref, short_ref, long_ref, mixed, corr = rest
    if first > 0:
        head_ref[:, :, :first] = earlier[...]
    groups = LANES // GROUP
    lane = lax.broadcasted_iota(jnp.int32, (1, LANES), 1)
    owner = lane // GROUP
    upside = (
        lax.broadcasted_iota(jnp.int32, (ROWS, ROWS), 0) ^ (PIECE - 1)
        == lax.broadcasted_iota(jnp.int32, (ROWS, ROWS), 1)
    ).astype(F32).astype(BF)
    owners = [(owner == g).astype(F32).astype(BF) for g in range(groups)]
    owners = [jnp.concatenate([m, m], axis=1) for m in owners]

    def one(t, here):
        tile = first // LANES + here
        cols = lanes_of(here)
        skip = taps_of(table, tile * 3)[7:8]
        forward = fw[tile, :, :SPAN]
        backward = bw[tile, :, :SPAN]
        product = prod[:, cols]
        gated = gate[:, cols]
        context = jnp.concatenate([prior[:, cols], product], axis=0)
        coming = jnp.concatenate([gated, ahead[:, cols]], axis=0)
        turned = jnp.dot(upside, product, preferred_element_type=F32).astype(BF)
        wave, prod_grad = [], []
        lagged = None
        for pair in range(ROWS // (2 * PIECE)):
            low = 2 * PIECE * pair
            result = jnp.dot(forward, windows(context, pair), preferred_element_type=F32)
            wave += [picked(result[:, :LANES], owner), picked(result[:, LANES:], owner)]
            seen = windows(coming, pair)
            result = jnp.dot(backward, seen, preferred_element_type=F32)
            prod_grad += [picked(result[:, :LANES], owner), picked(result[:, LANES:], owner)]
            own = jnp.concatenate([turned[low : low + PIECE], turned[low + PIECE : low + 2 * PIECE]], axis=1)
            masked = jnp.concatenate([own * m for m in owners], axis=0)
            term = lax.dot_general(masked, seen, (((1,), (1,)), ((), ())), preferred_element_type=F32)
            lagged = term if lagged is None else lagged + term
        product = product.astype(F32)
        gated = gated.astype(F32)
        wave = jnp.concatenate(wave, axis=0) + skip * product
        prod_grad = jnp.concatenate(prod_grad, axis=0) + skip * gated
        corr[t, :, :SPAN] = lagged
        for g in range(groups):
            skewed = pltpu.roll(
                corr[t, g * PIECE : (g + 1) * PIECE, :], 2 * LANES - PIECE + 1, 1, stride=1, stride_axis=0
            )
            long_ref[here, g : g + 1, :] = jnp.sum(skewed[:, :LANES], axis=0, keepdims=True)
        long_ref[here, 8:9, :] = jnp.sum(gated * product, axis=0, keepdims=True)
        long_ref[here, 9:16, :] = jnp.zeros((7, LANES), F32)
        features = (
            cot[0, :, lanes_of(tile)].astype(F32) * wave,
            prod_grad * val[:, cols].astype(F32),
            prod_grad * key[:, cols].astype(F32),
        )
        for part in range(3):
            whence = lanes_of(tile + part * count)
            taps = taps_of(table, tile + part * count)
            feature = features[part]
            shifted = mixed.at[t, part]
            shifted[0:8, :] = jnp.zeros((8, LANES), F32)
            shifted[8 : 8 + ROWS, :] = feature
            shifted[8 + ROWS : 16 + ROWS, :] = jnp.zeros((8, LANES), F32)
            head_ref[part, :, lanes_of(tile)] = feature[0:8].astype(BF)
            early = before[:, whence].astype(F32)[8:16]
            values = streams[0, :, whence].astype(F32)
            totals = [None if lag == 0 else shifted[lag : lag + 8, :] * early for lag in range(SHORT)]
            done = []
            spread = [jnp.broadcast_to(taps[lag : lag + 1], (8, LANES)) for lag in range(SHORT)]
            for r in range(ROWS // 8):
                running = None
                value = values[r * 8 : (r + 1) * 8]
                for lag in range(SHORT):
                    moved = shifted[8 + r * 8 + lag : 16 + r * 8 + lag, :]
                    term = spread[lag] * moved
                    running = term if running is None else running + term
                    term = moved * value
                    totals[lag] = term if totals[lag] is None else totals[lag] + term
                done.append(running)
            running = jnp.concatenate(done, axis=0)
            sums = [jnp.sum(total, axis=0, keepdims=True) for total in totals]
            sums.append(jnp.zeros((1, LANES), F32))
            short_ref[part, here, :, :] = jnp.concatenate(sums, axis=0)
            gs_ref[part, :, cols] = running.astype(BF)
            tail_ref[part, here] = running[ROWS - 16 :]

    def some(step, _):
        for t in range(UNROLL):
            one(t, step * UNROLL + t)
        return 0

    for step in range(prod.shape[1] // LANES // UNROLL):
        some(step, 0)


def back(first, width, table, streams, before, grad_out, made, prior, ahead, filters, earlier):
    count = grad_out.shape[2] // LANES
    tiles = width // LANES
    outs = (
        jax.ShapeDtypeStruct((3, ROWS, width), BF),
        jax.ShapeDtypeStruct((3, tiles, 16, LANES), F32),
        jax.ShapeDtypeStruct((3, 8, first + width), BF),
        jax.ShapeDtypeStruct((3, tiles, 8, LANES), F32),
        jax.ShapeDtypeStruct((tiles, 16, LANES), F32),
    )
    return pl.pallas_call(
        functools.partial(back_kernel, first, count),
        out_shape=outs,
        in_specs=[whole()] * (12 + len(earlier)),
        out_specs=(whole(),) * len(outs),
        scratch_shapes=[
            pltpu.VMEM((UNROLL, 3, ROWS + 16, LANES), F32),
            pltpu.VMEM((UNROLL, 8 * PIECE, 2 * LANES), F32),
        ],
        compiler_params=params(FULL),
        cost_estimate=pl.CostEstimate(
            flops=600 * 3 * ROWS * width, bytes_accessed=24 * ROWS * width, transcendentals=0
        ),
        name="back",
    )(table, streams, before, grad_out, *made, prior, ahead, *filters, *earlier)


def finish_kernel(chunks, count, table, *refs):
    pieces, tails = refs[:chunks], refs[chunks : 2 * chunks]
    after, out_ref, strip, sems = refs[2 * chunks :]
    copies = []
    first = 0
    for c in range(chunks):
        width = pieces[c].shape[2]
        for part in range(3):
            start = part * count * LANES + first
            copies.append(
                pltpu.make_async_copy(
                    pieces[c].at[part, pl.ds(0, ROWS - 16), :],
                    out_ref.at[0, pl.ds(0, ROWS - 16), pl.ds(start, width)],
                    sems.at[3 * c + part],
                )
            )
            copies[-1].start()
        first += width
    first = 0
    for c in range(chunks):
        for part in range(3):
            for here in range(tails[c].shape[1]):
                tile = part * count + first + here
                taps = taps_of(table, tile)
                rows = after[part, :, lanes_of(first + here)].astype(F32)
                rows = jnp.concatenate([jnp.zeros((8, LANES), F32), rows], axis=0)
                tail = tails[c][part, here]
                last = tail[8:16]
                for lag in range(1, SHORT):
                    last = last + taps[lag : lag + 1] * rows[lag : lag + 8]
                strip[:, tile * LANES : (tile + 1) * LANES] = jnp.concatenate([tail[0:8], last], axis=0).astype(BF)
        first += tails[c].shape[1]
    copies.append(pltpu.make_async_copy(strip, out_ref.at[0, pl.ds(ROWS - 16, 16), :], sems.at[3 * chunks]))
    copies[-1].start()
    for copy in copies:
        copy.wait()


def finish(table, pieces, tails, after, shape):
    chunks = len(pieces)
    return pl.pallas_call(
        functools.partial(finish_kernel, chunks, shape[2] // LANES // 3),
        out_shape=jax.ShapeDtypeStruct(shape, BF),
        in_specs=[whole()] * (2 + 2 * chunks),
        out_specs=anywhere(),
        scratch_shapes=[pltpu.VMEM((16, shape[2]), BF), pltpu.SemaphoreType.DMA((3 * chunks + 1,))],
        compiler_params=params(FULL),
        cost_estimate=pl.CostEstimate(flops=10000000, bytes_accessed=2000000, transcendentals=0),
        name="finish",
    )(table, *pieces, *tails, after)


def bundle_kernel(chunks, shards, *refs):
    shorts, longs, out_ref = refs[:chunks], refs[chunks : 2 * chunks], refs[2 * chunks]
    where = [(c, i) for c in range(chunks) for i in range(longs[c].shape[0])]

    def short(tile):
        c, i = where[tile % shards]
        return shorts[c][tile // shards, i]

    for d in range(shards):
        c, i = where[d]
        long = longs[c][i]
        rows = [short(3 * d)[0:7], long[8:9], short(3 * d + 1), short(3 * d + 2), long[0:8]]
        out_ref[d] = jnp.concatenate(rows, axis=0).astype(BF)


def bundle(shorts, longs, shards):
    return pl.pallas_call(
        functools.partial(bundle_kernel, len(shorts), shards),
        out_shape=jax.ShapeDtypeStruct((shards, 32, LANES), BF),
        in_specs=[whole()] * (2 * len(shorts)),
        out_specs=whole(),
        compiler_params=params(FULL),
        name="bundle",
    )(*shorts, *longs)


def total_kernel(parts_ref, out_ref):
    out_ref[...] = jnp.broadcast_to(jnp.sum(parts_ref[...].astype(F32), axis=0).astype(BF)[None], out_ref.shape)


def total(parts, copies):
    return pl.pallas_call(
        total_kernel,
        out_shape=jax.ShapeDtypeStruct((copies,) + parts.shape[1:], BF),
        in_specs=[whole()],
        out_specs=whole(),
        compiler_params=params(FULL),
        name="total",
    )(parts)


def spread_kernel(scale, parts_ref, short_ref, long_ref, skip_ref):
    summed = jnp.sum(parts_ref[...].astype(F32), axis=0) * scale
    for part in range(3):
        short_ref[:, part * LANES : (part + 1) * LANES] = summed[8 * part : 8 * part + SHORT]
    long_ref[...] = summed[24:32]
    skip_ref[...] = summed[7:8]


def spread(parts, scale):
    return pl.pallas_call(
        functools.partial(spread_kernel, scale),
        out_shape=(
            jax.ShapeDtypeStruct((SHORT, 3 * LANES), F32),
            jax.ShapeDtypeStruct((8, LANES), F32),
            jax.ShapeDtypeStruct((1, LANES), F32),
        ),
        in_specs=[whole()],
        out_specs=(whole(),) * 3,
        compiler_params=params(FULL),
        name="spread",
    )(parts)


def passed_along(block, axis, distance):
    devices = range(lax.axis_size(axis))
    route = [(i - distance, i) for i in devices if i - distance in devices]
    return lax.ppermute(block, axis, route)


CHUNKS = (2560, 1536)


def local(streams, short_filter, long_filter, skip, grad_out):
    shards = lax.axis_size("dp")
    ring = lax.axis_size("seq")
    payload, tail_rows = pack(short_filter, long_filter, skip, streams, shards)
    before = passed_along(tail_rows, "seq", 1)
    gathered = lax.all_to_all(payload, "dp", 0, 0, tiled=True)
    work = []
    table, first = gathered, 0
    for width in CHUNKS:
        made = gates(first, width, table, streams, before, grad_out, first == 0)
        if first == 0:
            table = made[4]
        work.append((first, width, made[:4], passed_along(made[0], "seq", 1), passed_along(made[1], "seq", -1)))
        first += width
    filters = bands(table)
    done = []
    for first, width, made, prior, ahead in work:
        earlier = [done[-1][2]] if done else []
        done.append(back(first, width, table, streams, before, grad_out, made, prior, ahead, filters, earlier))
    pieces, tails, heads, shorts, longs = zip(*done)
    after = passed_along(heads[-1], "seq", -1)
    parts = total(lax.all_to_all(bundle(shorts, longs, shards), "dp", 0, 0, tiled=True), ring)
    parts = lax.all_to_all(parts, "seq", 0, 0, tiled=True)
    scale = 1.0 / math.sqrt(shards * ring * streams.shape[1])
    grad_short, grad_long, grad_skip = spread(parts, scale)
    grads = finish(table, pieces, tails, after, streams.shape)
    return grads, grad_short, grad_long, grad_skip[0]


def solution(mesh):
    placed = (P("dp", "seq", None), P(None, "dp"), P("dp", None), P("dp"), P("dp", "seq", None))
    return jax.shard_map(
        local,
        mesh=mesh,
        in_specs=placed,
        out_specs=(P("dp", "seq", None), P(None, "dp"), P("dp", None), P("dp")),
        check_vma=False,
    )
```

```python
import functools
import math

import jax
import jax.numpy as jnp
from jax import lax
from jax.experimental import pallas as pl
from jax.experimental.pallas import tpu as pltpu
from jax.sharding import PartitionSpec as P

LANES = 128
GROUP = 16
SHORT = 7
ROWS = 128
FULL = 6
UNROLL = 4
PIECE = 16
SPAN = PIECE + 128
BF = jnp.bfloat16
F32 = jnp.float32


def params(mib):
    return pltpu.CompilerParams(vmem_limit_bytes=mib * 1024 * 1024)


def lasting(us):
    return pl.CostEstimate(flops=int(us * 1.1e9), bytes_accessed=0, transcendentals=0)


def whole():
    return pl.BlockSpec(memory_space=pltpu.VMEM)


def in_hbm(array):
    return pltpu.with_memory_space_constraint(array, pltpu.HBM)


def anywhere():
    return pl.BlockSpec(memory_space=pl.ANY)


def pack_kernel(short_ref, long_ref, skip_ref, streams_ref, out_ref, tail_ref):
    tail_ref[...] = streams_ref[0]
    short = short_ref[...].astype(F32)
    skip = skip_ref[...].astype(F32)
    nothing = jnp.zeros((1, LANES), F32)
    rows = []
    for part in range(3):
        rows.append(short[:, part * LANES : (part + 1) * LANES])
        rows.append(skip if part == 0 else nothing)
    packed = jnp.concatenate(rows + [long_ref[...].astype(F32)], axis=0).astype(BF)
    out_ref[...] = jnp.broadcast_to(packed[None], out_ref.shape)


def pack(short_filter, long_filter, skip, streams, shards):
    return pl.pallas_call(
        pack_kernel,
        out_shape=(
            jax.ShapeDtypeStruct((shards, 32, LANES), BF),
            jax.ShapeDtypeStruct((16, streams.shape[2]), BF),
        ),
        in_specs=[
            pl.BlockSpec(short_filter.shape, lambda i: (0, 0)),
            pl.BlockSpec(long_filter.shape, lambda i: (0, 0)),
            pl.BlockSpec((1, LANES), lambda i: (0, 0)),
            pl.BlockSpec((1, 16, streams.shape[2]), lambda i: (0, ROWS // 16 - 1, 0)),
        ],
        out_specs=(
            pl.BlockSpec((shards, 32, LANES), lambda i: (0, 0, 0)),
            pl.BlockSpec((16, streams.shape[2]), lambda i: (0, 0)),
        ),
        grid=(1,),
        compiler_params=params(FULL),
        name="pack",
    )(*(in_hbm(x) for x in (short_filter, long_filter, skip[None], streams)))


def taps_of(table, tile):
    return table[tile // 3, pl.ds(pl.multiple_of(tile % 3 * 8, 8), 8), :]


def lanes_of(tile):
    start = tile * LANES
    return pl.ds(start if isinstance(start, int) else pl.multiple_of(start, LANES), LANES)


def mixture(slot, halo, source, taps):
    slot[0:8, :] = halo
    slot[8 : 8 + ROWS, :] = source.astype(F32)
    running = taps[0:1] * slot[8 : 8 + ROWS, :]
    for lag in range(1, SHORT):
        running = running + taps[lag : lag + 1] * slot[8 - lag : 8 - lag + ROWS, :]
    return running


def gates_kernel(first, lead, count, g_ref, streams, before, cot_hbm, *rest):
    rest = rest if lead else rest[1:]
    if lead:
        prod, gate, key, val, table, ext, cot, sem = rest
        table[...] = g_ref[...].astype(F32)
    else:
        prod, gate, key, val, ext, cot, sem = rest
        table = g_ref
    width = prod.shape[1]
    copy = pltpu.make_async_copy(cot_hbm.at[0, :, pl.ds(first, width)], cot, sem)
    copy.start()

    def feature(part, here):
        tile = first // LANES + here + part * count
        whence = lanes_of(tile)
        return mixture(
            ext.at[here % UNROLL, part], before[:, whence].astype(F32)[8:16], streams[0, :, whence], taps_of(table, tile)
        )

    for here in range(width // LANES):
        cols = lanes_of(here)
        keys, values = feature(1, here), feature(2, here)
        prod[:, cols] = (keys * values).astype(BF)
        key[:, cols] = keys.astype(BF)
        val[:, cols] = values.astype(BF)
    copy.wait()
    for here in range(width // LANES):
        cols = lanes_of(here)
        gate[:, cols] = (cot[:, cols].astype(F32) * feature(0, here)).astype(BF)


def gates(first, width, table, streams, before, grad_out, *later):
    count = grad_out.shape[2] // LANES
    lead = not later
    outs = [jax.ShapeDtypeStruct((ROWS, width), BF)] * 4
    if lead:
        outs.append(jax.ShapeDtypeStruct(table.shape, F32))
    return pl.pallas_call(
        functools.partial(gates_kernel, first, lead, count),
        out_shape=tuple(outs),
        in_specs=[whole()] * 3 + [anywhere()] * (1 + len(later)),
        out_specs=(whole(),) * len(outs),
        scratch_shapes=[
            pltpu.VMEM((UNROLL, 3, 8 + ROWS, LANES), F32),
            pltpu.VMEM((ROWS, width), BF),
            pltpu.SemaphoreType.DMA,
        ],
        compiler_params=params(FULL),
        cost_estimate=lasting(width / 1024),
        name="gates",
    )(table, streams, before, in_hbm(grad_out), *later)


def windows(block, pair):
    low = 2 * PIECE * pair
    return jnp.concatenate(
        [block[low : low + SPAN], block[low + PIECE : low + PIECE + SPAN]], axis=1
    )


def picked(result, owner):
    out = result[0:PIECE]
    for g in range(1, LANES // GROUP):
        out = jnp.where(owner == g, result[g * PIECE : (g + 1) * PIECE], out)
    return out


def toeplitz_rows(filters, shift):
    pieces = []
    for g in range(LANES // GROUP):
        line = jnp.concatenate([filters[g : g + 1], jnp.zeros((1, LANES), F32)], axis=1)
        line = jnp.broadcast_to(line, (PIECE, 2 * LANES))
        pieces.append(pltpu.roll(line, shift, 1, stride=1, stride_axis=0))
    return jnp.concatenate(pieces, axis=0).astype(BF)


def bands_kernel(tiles, g_ref, forward_ref, backward_ref):
    step = pl.program_id(0)
    flip = (
        lax.broadcasted_iota(jnp.int32, (LANES, LANES), 0)
        + lax.broadcasted_iota(jnp.int32, (LANES, LANES), 1)
        == LANES - 1
    ).astype(F32).astype(BF)
    for t in range(tiles):
        filters = g_ref[step * tiles + t, 24:32, :]
        flipped = jnp.dot(filters.astype(BF), flip, preferred_element_type=F32)
        forward_ref[t] = toeplitz_rows(flipped, 1)
        backward_ref[t] = toeplitz_rows(filters, 0)


def bands(gathered):
    shards = gathered.shape[0]
    tiles = 8
    out = jax.ShapeDtypeStruct((shards, LANES, 2 * LANES), BF)
    spec = pl.BlockSpec((tiles, LANES, 2 * LANES), lambda i: (i, 0, 0))
    return pl.pallas_call(
        functools.partial(bands_kernel, tiles),
        grid=(shards // tiles,),
        out_shape=(out, out),
        in_specs=[pl.BlockSpec(gathered.shape, lambda i: (0, 0, 0))],
        out_specs=(spec, spec),
        compiler_params=params(FULL),
        cost_estimate=lasting(1.4),
        name="bands",
    )(gathered)


def back_kernel(
    first, count, table, streams, before, cot, prod, gate, key, val, prior, ahead, fw, bw, *rest
):
    if first > 0:
        earlier, *rest = rest
    gs_ref, tail_ref, head_ref, short_ref, long_ref, mixed, corr = rest
    if first > 0:
        head_ref[:, :, :first] = earlier[...]
    groups = LANES // GROUP
    lane = lax.broadcasted_iota(jnp.int32, (1, LANES), 1)
    owner = lane // GROUP
    upside = (
        lax.broadcasted_iota(jnp.int32, (ROWS, ROWS), 0) ^ (PIECE - 1)
        == lax.broadcasted_iota(jnp.int32, (ROWS, ROWS), 1)
    ).astype(F32).astype(BF)
    owners = [(owner == g).astype(F32).astype(BF) for g in range(groups)]
    owners = [jnp.concatenate([m, m], axis=1) for m in owners]

    def one(t, here):
        tile = first // LANES + here
        cols = lanes_of(here)
        skip = taps_of(table, tile * 3)[7:8]
        forward = fw[tile, :, :SPAN]
        backward = bw[tile, :, :SPAN]
        product = prod[:, cols]
        gated = gate[:, cols]
        context = jnp.concatenate([prior[:, cols], product], axis=0)
        coming = jnp.concatenate([gated, ahead[:, cols]], axis=0)
        turned = jnp.dot(upside, product, preferred_element_type=F32).astype(BF)
        wave, prod_grad = [], []
        lagged = None
        for pair in range(ROWS // (2 * PIECE)):
            low = 2 * PIECE * pair
            result = jnp.dot(forward, windows(context, pair), preferred_element_type=F32)
            wave += [picked(result[:, :LANES], owner), picked(result[:, LANES:], owner)]
            seen = windows(coming, pair)
            result = jnp.dot(backward, seen, preferred_element_type=F32)
            prod_grad += [picked(result[:, :LANES], owner), picked(result[:, LANES:], owner)]
            own = jnp.concatenate([turned[low : low + PIECE], turned[low + PIECE : low + 2 * PIECE]], axis=1)
            masked = jnp.concatenate([own * m for m in owners], axis=0)
            term = lax.dot_general(masked, seen, (((1,), (1,)), ((), ())), preferred_element_type=F32)
            lagged = term if lagged is None else lagged + term
        product = product.astype(F32)
        gated = gated.astype(F32)
        wave = jnp.concatenate(wave, axis=0) + skip * product
        prod_grad = jnp.concatenate(prod_grad, axis=0) + skip * gated
        corr[t, :, :SPAN] = lagged
        for g in range(groups):
            skewed = pltpu.roll(
                corr[t, g * PIECE : (g + 1) * PIECE, :], 2 * LANES - PIECE + 1, 1, stride=1, stride_axis=0
            )
            long_ref[here, g : g + 1, :] = jnp.sum(skewed[:, :LANES], axis=0, keepdims=True)
        long_ref[here, 8:9, :] = jnp.sum(gated * product, axis=0, keepdims=True)
        long_ref[here, 9:16, :] = jnp.zeros((7, LANES), F32)
        features = (
            cot[0, :, lanes_of(tile)].astype(F32) * wave,
            prod_grad * val[:, cols].astype(F32),
            prod_grad * key[:, cols].astype(F32),
        )
        for part in range(3):
            whence = lanes_of(tile + part * count)
            taps = taps_of(table, tile + part * count)
            feature = features[part]
            shifted = mixed.at[t, part]
            shifted[0:8, :] = jnp.zeros((8, LANES), F32)
            shifted[8 : 8 + ROWS, :] = feature
            shifted[8 + ROWS : 16 + ROWS, :] = jnp.zeros((8, LANES), F32)
            head_ref[part, :, lanes_of(tile)] = feature[0:8].astype(BF)
            early = before[:, whence].astype(F32)[8:16]
            values = streams[0, :, whence].astype(F32)
            totals = [None if lag == 0 else shifted[lag : lag + 8, :] * early for lag in range(SHORT)]
            done = []
            spread = [jnp.broadcast_to(taps[lag : lag + 1], (8, LANES)) for lag in range(SHORT)]
            for r in range(ROWS // 8):
                running = None
                value = values[r * 8 : (r + 1) * 8]
                for lag in range(SHORT):
                    moved = shifted[8 + r * 8 + lag : 16 + r * 8 + lag, :]
                    term = spread[lag] * moved
                    running = term if running is None else running + term
                    term = moved * value
                    totals[lag] = term if totals[lag] is None else totals[lag] + term
                done.append(running)
            running = jnp.concatenate(done, axis=0)
            sums = [jnp.sum(total, axis=0, keepdims=True) for total in totals]
            sums.append(jnp.zeros((1, LANES), F32))
            short_ref[part, here, :, :] = jnp.concatenate(sums, axis=0)
            gs_ref[part, :, cols] = running.astype(BF)
            tail_ref[part, here] = running[ROWS - 16 :]

    def some(step, _):
        for t in range(UNROLL):
            one(t, step * UNROLL + t)
        return 0

    for step in range(prod.shape[1] // LANES // UNROLL):
        some(step, 0)


def back(first, width, table, streams, before, grad_out, made, prior, ahead, filters, earlier):
    count = grad_out.shape[2] // LANES
    tiles = width // LANES
    outs = (
        jax.ShapeDtypeStruct((3, ROWS, width), BF),
        jax.ShapeDtypeStruct((3, tiles, 16, LANES), F32),
        jax.ShapeDtypeStruct((3, 8, first + width), BF),
        jax.ShapeDtypeStruct((3, tiles, 8, LANES), F32),
        jax.ShapeDtypeStruct((tiles, 16, LANES), F32),
    )
    return pl.pallas_call(
        functools.partial(back_kernel, first, count),
        out_shape=outs,
        in_specs=[whole()] * (12 + len(earlier)),
        out_specs=(whole(),) * len(outs),
        scratch_shapes=[
            pltpu.VMEM((UNROLL, 3, ROWS + 16, LANES), F32),
            pltpu.VMEM((UNROLL, 8 * PIECE, 2 * LANES), F32),
        ],
        compiler_params=params(FULL),
        cost_estimate=lasting(3.4 * width / 1024),
        name="back",
    )(table, streams, before, grad_out, *made, prior, ahead, *filters, *earlier)


def finish_kernel(chunks, count, table, *refs):
    pieces, tails = refs[:chunks], refs[chunks : 2 * chunks]
    after, out_ref, strip, sems = refs[2 * chunks :]
    copies = []
    first = 0
    for c in range(chunks):
        width = pieces[c].shape[2]
        for part in range(3):
            start = part * count * LANES + first
            copies.append(
                pltpu.make_async_copy(
                    pieces[c].at[part, pl.ds(0, ROWS - 16), :],
                    out_ref.at[0, pl.ds(0, ROWS - 16), pl.ds(start, width)],
                    sems.at[3 * c + part],
                )
            )
            copies[-1].start()
        first += width
    first = 0
    for c in range(chunks):
        for part in range(3):
            for here in range(tails[c].shape[1]):
                tile = part * count + first + here
                taps = taps_of(table, tile)
                rows = after[part, :, lanes_of(first + here)].astype(F32)
                rows = jnp.concatenate([jnp.zeros((8, LANES), F32), rows], axis=0)
                tail = tails[c][part, here]
                last = tail[8:16]
                for lag in range(1, SHORT):
                    last = last + taps[lag : lag + 1] * rows[lag : lag + 8]
                strip[:, tile * LANES : (tile + 1) * LANES] = jnp.concatenate([tail[0:8], last], axis=0).astype(BF)
        first += tails[c].shape[1]
    copies.append(pltpu.make_async_copy(strip, out_ref.at[0, pl.ds(ROWS - 16, 16), :], sems.at[3 * chunks]))
    copies[-1].start()
    for copy in copies:
        copy.wait()


def finish(table, pieces, tails, after, shape):
    chunks = len(pieces)
    return pl.pallas_call(
        functools.partial(finish_kernel, chunks, shape[2] // LANES // 3),
        out_shape=jax.ShapeDtypeStruct(shape, BF),
        in_specs=[whole()] * (2 + 2 * chunks),
        out_specs=anywhere(),
        scratch_shapes=[pltpu.VMEM((16, shape[2]), BF), pltpu.SemaphoreType.DMA((3 * chunks + 1,))],
        compiler_params=params(FULL),
        cost_estimate=lasting(2.6),
        name="finish",
    )(table, *pieces, *tails, after)


def bundle_kernel(chunks, shards, *refs):
    shorts, longs, out_ref = refs[:chunks], refs[chunks : 2 * chunks], refs[2 * chunks]
    where = [(c, i) for c in range(chunks) for i in range(longs[c].shape[0])]

    def short(tile):
        c, i = where[tile % shards]
        return shorts[c][tile // shards, i]

    for d in range(shards):
        c, i = where[d]
        long = longs[c][i]
        rows = [short(3 * d)[0:7], long[8:9], short(3 * d + 1), short(3 * d + 2), long[0:8]]
        out_ref[d] = jnp.concatenate(rows, axis=0).astype(BF)


def bundle(shorts, longs, shards):
    return pl.pallas_call(
        functools.partial(bundle_kernel, len(shorts), shards),
        out_shape=jax.ShapeDtypeStruct((shards, 32, LANES), BF),
        in_specs=[whole()] * (2 * len(shorts)),
        out_specs=whole(),
        compiler_params=params(FULL),
        name="bundle",
    )(*shorts, *longs)


def total_kernel(parts_ref, out_ref):
    out_ref[...] = jnp.broadcast_to(jnp.sum(parts_ref[...].astype(F32), axis=0).astype(BF)[None], out_ref.shape)


def total(parts, copies):
    return pl.pallas_call(
        total_kernel,
        out_shape=jax.ShapeDtypeStruct((copies,) + parts.shape[1:], BF),
        in_specs=[whole()],
        out_specs=whole(),
        compiler_params=params(FULL),
        name="total",
    )(parts)


def spread_kernel(scale, parts_ref, short_ref, long_ref, skip_ref):
    summed = jnp.sum(parts_ref[...].astype(F32), axis=0) * scale
    for part in range(3):
        short_ref[:, part * LANES : (part + 1) * LANES] = summed[8 * part : 8 * part + SHORT]
    long_ref[...] = summed[24:32]
    skip_ref[...] = summed[7:8]


def spread(parts, scale):
    return pl.pallas_call(
        functools.partial(spread_kernel, scale),
        out_shape=(
            jax.ShapeDtypeStruct((SHORT, 3 * LANES), F32),
            jax.ShapeDtypeStruct((8, LANES), F32),
            jax.ShapeDtypeStruct((1, LANES), F32),
        ),
        in_specs=[whole()],
        out_specs=(whole(),) * 3,
        compiler_params=params(FULL),
        name="spread",
    )(parts)


def passed_along(block, axis, distance):
    devices = range(lax.axis_size(axis))
    route = [(i - distance, i) for i in devices if i - distance in devices]
    return lax.ppermute(block, axis, route)


CHUNKS = (2560, 1536)


def local(streams, short_filter, long_filter, skip, grad_out):
    shards = lax.axis_size("dp")
    ring = lax.axis_size("seq")
    payload, tail_rows = pack(short_filter, long_filter, skip, streams, shards)
    before = passed_along(tail_rows, "seq", 1)
    gathered = lax.all_to_all(payload, "dp", 0, 0, tiled=True)
    work = []
    table, first, filters = gathered, 0, ()
    for width in CHUNKS:
        made = gates(first, width, table, streams, before, grad_out, *filters[:1])
        if first == 0:
            table = made[4]
            filters = bands(table)
        work.append((first, width, made[:4], passed_along(made[0], "seq", 1), passed_along(made[1], "seq", -1)))
        first += width
    done = []
    for first, width, made, prior, ahead in work:
        earlier = [done[-1][2]] if done else []
        done.append(back(first, width, table, streams, before, grad_out, made, prior, ahead, filters, earlier))
    pieces, tails, heads, shorts, longs = zip(*done)
    after = passed_along(heads[-1], "seq", -1)
    parts = total(lax.all_to_all(bundle(shorts, longs, shards), "dp", 0, 0, tiled=True), ring)
    parts = lax.all_to_all(parts, "seq", 0, 0, tiled=True)
    scale = 1.0 / math.sqrt(shards * ring * streams.shape[1])
    grad_short, grad_long, grad_skip = spread(parts, scale)
    grads = finish(table, pieces, tails, after, streams.shape)
    return grads, grad_short, grad_long, grad_skip[0]


def solution(mesh):
    placed = (P("dp", "seq", None), P(None, "dp"), P("dp", None), P("dp"), P("dp", "seq", None))
    return jax.shard_map(
        local,
        mesh=mesh,
        in_specs=placed,
        out_specs=(P("dp", "seq", None), P(None, "dp"), P("dp", None), P("dp")),
        check_vma=False,
    )
```

```python
import functools
import math

import jax
import jax.numpy as jnp
from jax import lax
from jax.experimental import pallas as pl
from jax.experimental.pallas import tpu as pltpu
from jax.sharding import PartitionSpec as P

LANES = 128
GROUP = 16
SHORT = 7
ROWS = 128
FULL = 6
UNROLL = 4
PIECE = 16
SPAN = PIECE + 128
BF = jnp.bfloat16
F32 = jnp.float32


def params(mib):
    return pltpu.CompilerParams(vmem_limit_bytes=mib * 1024 * 1024)


def lasting(us):
    return pl.CostEstimate(flops=int(us * 1.1e9), bytes_accessed=0, transcendentals=0)


def whole():
    return pl.BlockSpec(memory_space=pltpu.VMEM)


def in_hbm(array):
    return pltpu.with_memory_space_constraint(array, pltpu.HBM)


def anywhere():
    return pl.BlockSpec(memory_space=pl.ANY)


def pack_kernel(short_ref, long_ref, skip_ref, streams_ref, out_ref, tail_ref):
    tail_ref[...] = streams_ref[0]
    short = short_ref[...].astype(F32)
    skip = skip_ref[...].astype(F32)
    nothing = jnp.zeros((1, LANES), F32)
    rows = []
    for part in range(3):
        rows.append(short[:, part * LANES : (part + 1) * LANES])
        rows.append(skip if part == 0 else nothing)
    packed = jnp.concatenate(rows + [long_ref[...].astype(F32)], axis=0).astype(BF)
    out_ref[...] = jnp.broadcast_to(packed[None], out_ref.shape)


def pack(short_filter, long_filter, skip, streams, shards):
    return pl.pallas_call(
        pack_kernel,
        out_shape=(
            jax.ShapeDtypeStruct((shards, 32, LANES), BF),
            jax.ShapeDtypeStruct((16, streams.shape[2]), BF),
        ),
        in_specs=[
            pl.BlockSpec(short_filter.shape, lambda i: (0, 0)),
            pl.BlockSpec(long_filter.shape, lambda i: (0, 0)),
            pl.BlockSpec((1, LANES), lambda i: (0, 0)),
            pl.BlockSpec((1, 16, streams.shape[2]), lambda i: (0, ROWS // 16 - 1, 0)),
        ],
        out_specs=(
            pl.BlockSpec((shards, 32, LANES), lambda i: (0, 0, 0)),
            pl.BlockSpec((16, streams.shape[2]), lambda i: (0, 0)),
        ),
        grid=(1,),
        compiler_params=params(FULL),
        name="pack",
    )(*(in_hbm(x) for x in (short_filter, long_filter, skip[None], streams)))


def taps_of(table, tile):
    return table[tile // 3, pl.ds(pl.multiple_of(tile % 3 * 8, 8), 8), :]


def lanes_of(tile):
    start = tile * LANES
    return pl.ds(start if isinstance(start, int) else pl.multiple_of(start, LANES), LANES)


def mixture(slot, halo, source, taps):
    slot[0:8, :] = halo
    slot[8 : 8 + ROWS, :] = source.astype(F32)
    running = taps[0:1] * slot[8 : 8 + ROWS, :]
    for lag in range(1, SHORT):
        running = running + taps[lag : lag + 1] * slot[8 - lag : 8 - lag + ROWS, :]
    return running


def gates_kernel(first, lead, count, g_ref, streams, before, cot_hbm, *rest):
    rest = rest if lead else rest[1:]
    if lead:
        prod, gate, key, val, table, ext, cot, sem = rest
        table[...] = g_ref[...].astype(F32)
    else:
        prod, gate, key, val, ext, cot, sem = rest
        table = g_ref
    width = prod.shape[1]
    copy = pltpu.make_async_copy(cot_hbm.at[0, :, pl.ds(first, width)], cot, sem)
    copy.start()

    def feature(part, here):
        tile = first // LANES + here + part * count
        whence = lanes_of(tile)
        return mixture(
            ext.at[here % UNROLL, part], before[:, whence].astype(F32)[8:16], streams[0, :, whence], taps_of(table, tile)
        )

    for here in range(width // LANES):
        cols = lanes_of(here)
        keys, values = feature(1, here), feature(2, here)
        prod[:, cols] = (keys * values).astype(BF)
        key[:, cols] = keys.astype(BF)
        val[:, cols] = values.astype(BF)
    copy.wait()
    for here in range(width // LANES):
        cols = lanes_of(here)
        gate[:, cols] = (cot[:, cols].astype(F32) * feature(0, here)).astype(BF)


def gates(first, width, table, streams, before, grad_out, *later):
    count = grad_out.shape[2] // LANES
    lead = not later
    outs = [jax.ShapeDtypeStruct((ROWS, width), BF)] * 4
    if lead:
        outs.append(jax.ShapeDtypeStruct(table.shape, F32))
    return pl.pallas_call(
        functools.partial(gates_kernel, first, lead, count),
        out_shape=tuple(outs),
        in_specs=[whole()] * 3 + [anywhere()] * (1 + len(later)),
        out_specs=(whole(),) * len(outs),
        scratch_shapes=[
            pltpu.VMEM((UNROLL, 3, 8 + ROWS, LANES), F32),
            pltpu.VMEM((ROWS, width), BF),
            pltpu.SemaphoreType.DMA,
        ],
        compiler_params=params(FULL),
        cost_estimate=lasting(width / 1024),
        name="gates",
    )(table, streams, before, in_hbm(grad_out), *later)


def windows(block, pair):
    low = 2 * PIECE * pair
    return jnp.concatenate(
        [block[low : low + SPAN], block[low + PIECE : low + PIECE + SPAN]], axis=1
    )


def picked(result, bits):
    parts = [result[g * PIECE : (g + 1) * PIECE] for g in range(LANES // GROUP)]
    for bit in bits:
        parts = [jnp.where(bit, parts[k + 1], parts[k]) for k in range(0, len(parts), 2)]
    return parts[0]


def toeplitz_rows(filters, shift):
    pieces = []
    for g in range(LANES // GROUP):
        line = jnp.concatenate([filters[g : g + 1], jnp.zeros((1, LANES), F32)], axis=1)
        line = jnp.broadcast_to(line, (PIECE, 2 * LANES))
        pieces.append(pltpu.roll(line, shift, 1, stride=1, stride_axis=0))
    return jnp.concatenate(pieces, axis=0).astype(BF)


def bands_kernel(tiles, g_ref, forward_ref, backward_ref):
    step = pl.program_id(0)
    flip = (
        lax.broadcasted_iota(jnp.int32, (LANES, LANES), 0)
        + lax.broadcasted_iota(jnp.int32, (LANES, LANES), 1)
        == LANES - 1
    ).astype(F32).astype(BF)
    for t in range(tiles):
        filters = g_ref[step * tiles + t, 24:32, :]
        flipped = jnp.dot(filters.astype(BF), flip, preferred_element_type=F32)
        forward_ref[t] = toeplitz_rows(flipped, 1)
        backward_ref[t] = toeplitz_rows(filters, 0)


def bands(gathered):
    shards = gathered.shape[0]
    tiles = 8
    out = jax.ShapeDtypeStruct((shards, LANES, 2 * LANES), BF)
    spec = pl.BlockSpec((tiles, LANES, 2 * LANES), lambda i: (i, 0, 0))
    return pl.pallas_call(
        functools.partial(bands_kernel, tiles),
        grid=(shards // tiles,),
        out_shape=(out, out),
        in_specs=[pl.BlockSpec(gathered.shape, lambda i: (0, 0, 0))],
        out_specs=(spec, spec),
        compiler_params=params(FULL),
        cost_estimate=lasting(1.4),
        name="bands",
    )(gathered)


def back_kernel(
    first, count, table, streams, before, cot, prod, gate, key, val, prior, ahead, fw, bw, *rest
):
    if first > 0:
        earlier, *rest = rest
    gs_ref, tail_ref, head_ref, short_ref, long_ref, mixed, corr = rest
    if first > 0:
        head_ref[:, :, :first] = earlier[...]
    groups = LANES // GROUP
    lane = lax.broadcasted_iota(jnp.int32, (1, LANES), 1)
    owner = lane // GROUP
    place = lax.broadcasted_iota(jnp.int32, (PIECE, LANES), 1) // GROUP
    bits = [(place >> k) % 2 == 1 for k in range(3)]
    upside = (
        lax.broadcasted_iota(jnp.int32, (ROWS, ROWS), 0) ^ (PIECE - 1)
        == lax.broadcasted_iota(jnp.int32, (ROWS, ROWS), 1)
    ).astype(F32).astype(BF)
    owners = [(owner == g).astype(F32).astype(BF) for g in range(groups)]
    owners = [jnp.concatenate([m, m], axis=1) for m in owners]

    def one(t, here):
        tile = first // LANES + here
        cols = lanes_of(here)
        skip = taps_of(table, tile * 3)[7:8]
        forward = fw[tile, :, :SPAN]
        backward = bw[tile, :, :SPAN]
        product = prod[:, cols]
        gated = gate[:, cols]
        context = jnp.concatenate([prior[:, cols], product], axis=0)
        coming = jnp.concatenate([gated, ahead[:, cols]], axis=0)
        turned = jnp.dot(upside, product, preferred_element_type=F32).astype(BF)
        wave, prod_grad = [], []
        lagged = None
        for pair in range(ROWS // (2 * PIECE)):
            low = 2 * PIECE * pair
            result = jnp.dot(forward, windows(context, pair), preferred_element_type=F32)
            wave += [picked(result[:, :LANES], bits), picked(result[:, LANES:], bits)]
            seen = windows(coming, pair)
            result = jnp.dot(backward, seen, preferred_element_type=F32)
            prod_grad += [picked(result[:, :LANES], bits), picked(result[:, LANES:], bits)]
            own = jnp.concatenate([turned[low : low + PIECE], turned[low + PIECE : low + 2 * PIECE]], axis=1)
            masked = jnp.concatenate([own * m for m in owners], axis=0)
            term = lax.dot_general(masked, seen, (((1,), (1,)), ((), ())), preferred_element_type=F32)
            lagged = term if lagged is None else lagged + term
        product = product.astype(F32)
        gated = gated.astype(F32)
        wave = jnp.concatenate(wave, axis=0) + skip * product
        prod_grad = jnp.concatenate(prod_grad, axis=0) + skip * gated
        corr[t, :, :SPAN] = lagged
        for g in range(groups):
            skewed = pltpu.roll(
                corr[t, g * PIECE : (g + 1) * PIECE, :], 2 * LANES - PIECE + 1, 1, stride=1, stride_axis=0
            )
            long_ref[here, g : g + 1, :] = jnp.sum(skewed[:, :LANES], axis=0, keepdims=True)
        long_ref[here, 8:9, :] = jnp.sum(gated * product, axis=0, keepdims=True)
        long_ref[here, 9:16, :] = jnp.zeros((7, LANES), F32)
        features = (
            cot[0, :, lanes_of(tile)].astype(F32) * wave,
            prod_grad * val[:, cols].astype(F32),
            prod_grad * key[:, cols].astype(F32),
        )
        for part in range(3):
            whence = lanes_of(tile + part * count)
            taps = taps_of(table, tile + part * count)
            feature = features[part]
            shifted = mixed.at[t, part]
            shifted[0:8, :] = jnp.zeros((8, LANES), F32)
            shifted[8 : 8 + ROWS, :] = feature
            shifted[8 + ROWS : 16 + ROWS, :] = jnp.zeros((8, LANES), F32)
            head_ref[part, :, lanes_of(tile)] = feature[0:8].astype(BF)
            early = before[:, whence].astype(F32)[8:16]
            values = streams[0, :, whence].astype(F32)
            totals = [None if lag == 0 else shifted[lag : lag + 8, :] * early for lag in range(SHORT)]
            done = []
            spread = [jnp.broadcast_to(taps[lag : lag + 1], (8, LANES)) for lag in range(SHORT)]
            for r in range(ROWS // 8):
                running = None
                value = values[r * 8 : (r + 1) * 8]
                for lag in range(SHORT):
                    moved = shifted[8 + r * 8 + lag : 16 + r * 8 + lag, :]
                    term = spread[lag] * moved
                    running = term if running is None else running + term
                    term = moved * value
                    totals[lag] = term if totals[lag] is None else totals[lag] + term
                done.append(running)
            running = jnp.concatenate(done, axis=0)
            sums = [jnp.sum(total, axis=0, keepdims=True) for total in totals]
            sums.append(jnp.zeros((1, LANES), F32))
            short_ref[part, here, :, :] = jnp.concatenate(sums, axis=0)
            gs_ref[part, :, cols] = running.astype(BF)
            tail_ref[part, here] = running[ROWS - 16 :]

    def some(step, _):
        for t in range(UNROLL):
            one(t, step * UNROLL + t)
        return 0

    for step in range(prod.shape[1] // LANES // UNROLL):
        some(step, 0)


def back(first, width, table, streams, before, grad_out, made, prior, ahead, filters, earlier):
    count = grad_out.shape[2] // LANES
    tiles = width // LANES
    outs = (
        jax.ShapeDtypeStruct((3, ROWS, width), BF),
        jax.ShapeDtypeStruct((3, tiles, 16, LANES), F32),
        jax.ShapeDtypeStruct((3, 8, first + width), BF),
        jax.ShapeDtypeStruct((3, tiles, 8, LANES), F32),
        jax.ShapeDtypeStruct((tiles, 16, LANES), F32),
    )
    return pl.pallas_call(
        functools.partial(back_kernel, first, count),
        out_shape=outs,
        in_specs=[whole()] * (12 + len(earlier)),
        out_specs=(whole(),) * len(outs),
        scratch_shapes=[
            pltpu.VMEM((UNROLL, 3, ROWS + 16, LANES), F32),
            pltpu.VMEM((UNROLL, 8 * PIECE, 2 * LANES), F32),
        ],
        compiler_params=params(FULL),
        cost_estimate=lasting(3.4 * width / 1024),
        name="back",
    )(table, streams, before, grad_out, *made, prior, ahead, *filters, *earlier)


def finish_kernel(chunks, count, table, *refs):
    pieces, tails = refs[:chunks], refs[chunks : 2 * chunks]
    after, out_ref, strip, sems = refs[2 * chunks :]
    copies = []
    first = 0
    for c in range(chunks):
        width = pieces[c].shape[2]
        for part in range(3):
            start = part * count * LANES + first
            copies.append(
                pltpu.make_async_copy(
                    pieces[c].at[part, pl.ds(0, ROWS - 16), :],
                    out_ref.at[0, pl.ds(0, ROWS - 16), pl.ds(start, width)],
                    sems.at[3 * c + part],
                )
            )
            copies[-1].start()
        first += width
    first = 0
    for c in range(chunks):
        for part in range(3):
            for here in range(tails[c].shape[1]):
                tile = part * count + first + here
                taps = taps_of(table, tile)
                rows = after[part, :, lanes_of(first + here)].astype(F32)
                rows = jnp.concatenate([jnp.zeros((8, LANES), F32), rows], axis=0)
                tail = tails[c][part, here]
                last = tail[8:16]
                for lag in range(1, SHORT):
                    last = last + taps[lag : lag + 1] * rows[lag : lag + 8]
                strip[:, tile * LANES : (tile + 1) * LANES] = jnp.concatenate([tail[0:8], last], axis=0).astype(BF)
        first += tails[c].shape[1]
    copies.append(pltpu.make_async_copy(strip, out_ref.at[0, pl.ds(ROWS - 16, 16), :], sems.at[3 * chunks]))
    copies[-1].start()
    for copy in copies:
        copy.wait()


def finish(table, pieces, tails, after, shape):
    chunks = len(pieces)
    return pl.pallas_call(
        functools.partial(finish_kernel, chunks, shape[2] // LANES // 3),
        out_shape=jax.ShapeDtypeStruct(shape, BF),
        in_specs=[whole()] * (2 + 2 * chunks),
        out_specs=anywhere(),
        scratch_shapes=[pltpu.VMEM((16, shape[2]), BF), pltpu.SemaphoreType.DMA((3 * chunks + 1,))],
        compiler_params=params(FULL),
        cost_estimate=lasting(2.6),
        name="finish",
    )(table, *pieces, *tails, after)


def bundle_kernel(chunks, shards, *refs):
    shorts, longs, out_ref = refs[:chunks], refs[chunks : 2 * chunks], refs[2 * chunks]
    where = [(c, i) for c in range(chunks) for i in range(longs[c].shape[0])]

    def short(tile):
        c, i = where[tile % shards]
        return shorts[c][tile // shards, i]

    for d in range(shards):
        c, i = where[d]
        long = longs[c][i]
        rows = [short(3 * d)[0:7], long[8:9], short(3 * d + 1), short(3 * d + 2), long[0:8]]
        out_ref[d] = jnp.concatenate(rows, axis=0).astype(BF)


def bundle(shorts, longs, shards):
    return pl.pallas_call(
        functools.partial(bundle_kernel, len(shorts), shards),
        out_shape=jax.ShapeDtypeStruct((shards, 32, LANES), BF),
        in_specs=[whole()] * (2 * len(shorts)),
        out_specs=whole(),
        compiler_params=params(FULL),
        name="bundle",
    )(*shorts, *longs)


def total_kernel(parts_ref, out_ref):
    out_ref[...] = jnp.broadcast_to(jnp.sum(parts_ref[...].astype(F32), axis=0).astype(BF)[None], out_ref.shape)


def total(parts, copies):
    return pl.pallas_call(
        total_kernel,
        out_shape=jax.ShapeDtypeStruct((copies,) + parts.shape[1:], BF),
        in_specs=[whole()],
        out_specs=whole(),
        compiler_params=params(FULL),
        name="total",
    )(parts)


def spread_kernel(scale, parts_ref, short_ref, long_ref, skip_ref):
    summed = jnp.sum(parts_ref[...].astype(F32), axis=0) * scale
    for part in range(3):
        short_ref[:, part * LANES : (part + 1) * LANES] = summed[8 * part : 8 * part + SHORT]
    long_ref[...] = summed[24:32]
    skip_ref[...] = summed[7:8]


def spread(parts, scale):
    return pl.pallas_call(
        functools.partial(spread_kernel, scale),
        out_shape=(
            jax.ShapeDtypeStruct((SHORT, 3 * LANES), F32),
            jax.ShapeDtypeStruct((8, LANES), F32),
            jax.ShapeDtypeStruct((1, LANES), F32),
        ),
        in_specs=[whole()],
        out_specs=(whole(),) * 3,
        compiler_params=params(FULL),
        name="spread",
    )(parts)


def passed_along(block, axis, distance):
    devices = range(lax.axis_size(axis))
    route = [(i - distance, i) for i in devices if i - distance in devices]
    return lax.ppermute(block, axis, route)


CHUNKS = (2560, 1536)


def local(streams, short_filter, long_filter, skip, grad_out):
    shards = lax.axis_size("dp")
    ring = lax.axis_size("seq")
    payload, tail_rows = pack(short_filter, long_filter, skip, streams, shards)
    before = passed_along(tail_rows, "seq", 1)
    gathered = lax.all_to_all(payload, "dp", 0, 0, tiled=True)
    work = []
    table, first, filters = gathered, 0, ()
    for width in CHUNKS:
        made = gates(first, width, table, streams, before, grad_out, *filters[:1])
        if first == 0:
            table = made[4]
            filters = bands(table)
        work.append((first, width, made[:4], passed_along(made[0], "seq", 1), passed_along(made[1], "seq", -1)))
        first += width
    done = []
    for first, width, made, prior, ahead in work:
        earlier = [done[-1][2]] if done else []
        done.append(back(first, width, table, streams, before, grad_out, made, prior, ahead, filters, earlier))
    pieces, tails, heads, shorts, longs = zip(*done)
    after = passed_along(heads[-1], "seq", -1)
    parts = total(lax.all_to_all(bundle(shorts, longs, shards), "dp", 0, 0, tiled=True), ring)
    parts = lax.all_to_all(parts, "seq", 0, 0, tiled=True)
    scale = 1.0 / math.sqrt(shards * ring * streams.shape[1])
    grad_short, grad_long, grad_skip = spread(parts, scale)
    grads = finish(table, pieces, tails, after, streams.shape)
    return grads, grad_short, grad_long, grad_skip[0]


def solution(mesh):
    placed = (P("dp", "seq", None), P(None, "dp"), P("dp", None), P("dp"), P("dp", "seq", None))
    return jax.shard_map(
        local,
        mesh=mesh,
        in_specs=placed,
        out_specs=(P("dp", "seq", None), P(None, "dp"), P("dp", None), P("dp")),
        check_vma=False,
    )
```
